32 devices in a mesh: lat: 4 (over x, core), lon: 4 (over z), lev: 2 (over y).
Axes of the slice: x: 2, y: 2, z: 4, core: 2. Of those that a mesh axis runs over, the one named last changes fastest.
Arguments:
- fields: float32 [32, 32, 4, 512], P('lat', 'lon', 'lev'), may hold values from -6 to 6
- gain: float32 [512], replicated, may hold values from 0.1 to 1.9
- w_qkv: float32 [512, 1536], replicated, may hold values from -2 to 2
- w_out: float32 [512, 512], replicated, may hold values from -0.25 to 0.25
- cotangent: float32 [32, 32, 4, 512], P('lat', 'lon', 'lev'), may hold values from -6 to 6
Outputs:
- output: float32 [32, 32, 4, 512], P('lat', 'lon', 'lev')
- grad_fields: float32 [32, 32, 4, 512], P('lat', 'lon', 'lev')
- grad_gain: float32 [512], replicated
- grad_qkv: float32 [512, 1536], replicated
- grad_w_out: float32 [512, 512], replicated
The draws below stay inside these ranges and needn't reach their ends.
All inputs are finite; a program needn't handle non-finite values.
Results may differ from the reference program's by a relative error of at most 0.0003.
Values sent between devices are 32-bit elements; how exact they have to be, the bound alone decides.
No kernel may reach another device: no remote copies, remote signals or barrier semaphores. Data moves between devices by JAX's collectives and lax.ppermute only.
A program may use at most 128 MiB of HBM per device.

```python
import jax
import jax.numpy as jnp
from jax import lax

D = 512
HEADS = 16
HEAD_DIM = 32
WIN_LAT = 7
WIN_LON = 7
WIN_LEV = 3
LAT = 32
LON = 32
LEV = 4
TOKENS = 4096


def draw_w_qkv(key, part):
    entries = jnp.clip(jax.random.normal(key, (D, 3 * D), jnp.float32), -4.0, 4.0)
    return entries * D ** (-0.5)


def block_levels(stream_key, extent, shards, smallest, high):
    def one(position, blocks):
        heights = jax.random.uniform(jax.random.fold_in(jax.random.fold_in(stream_key, 6), position), (blocks,), jnp.float32, smallest / len(shards), high / len(shards))
        return jnp.repeat(jnp.exp(heights), extent[position] // blocks).reshape((-1,) + (1,) * (len(extent) - position - 1))

    level = one(*shards[0])
    for cut in shards[1:]:
        level = level * one(*cut)
    return level


def normal_values(key, extent, scale, most, shards=(), kind=jnp.bfloat16):
    drawn = jax.random.normal(key, extent, jnp.float32) * scale
    if len(shards) > 0:
        drawn = block_levels(key, extent, shards, -0.22, 0.18) * drawn
    return jnp.clip(drawn, min=-most, max=most).astype(kind)


def setup_inputs(seed: int = 0) -> dict:
    splits = jax.random.split(jax.random.key(seed), 6)
    return {
        "fields": normal_values(splits[0], (LAT, LON, LEV, D), 1.0, 6.0, ((0, 4), (1, 4), (2, 2)), jnp.float32),
        "gain": jnp.clip(1.0 + 0.18 * jax.random.normal(splits[1], (D,), jnp.float32), 0.1, 1.9),
        "w_qkv": draw_w_qkv(jax.random.fold_in(splits[5], 71), 0),
        "w_out": normal_values(splits[3], (D, D), D ** -0.5, 0.25, (), jnp.float32),
        "cotangent": normal_values(splits[4], (LAT, LON, LEV, D), 1.0, 6.0, ((0, 4), (1, 4), (2, 2)), jnp.float32),
    }


HIGH = lax.Precision.HIGHEST
EPSILON = 1e-06

def attend(query, keyval):
    lat_reach = (WIN_LAT - 1) // 2
    lon_reach = (WIN_LON - 1) // 2
    lev_reach = (WIN_LEV - 1) // 2
    padded = jnp.pad(keyval, ((lat_reach, lat_reach), (0, 0), (lev_reach, lev_reach), (0, 0)))
    padded = jnp.concatenate([padded[:, LON - lon_reach:], padded, padded[:, :lon_reach]], axis=1)
    lat_place = jnp.arange(LAT, dtype=jnp.int32)
    lev_place = jnp.arange(LEV, dtype=jnp.int32)

    def score_row(carry, shift):
        block = lax.dynamic_slice_in_dim(padded, shift, LAT, 0)
        lat_fine = (lat_place + shift - lat_reach >= 0) & (lat_place + shift - lat_reach < LAT)
        collected = []
        for lon_step in range(WIN_LON):
            for lev_step in range(WIN_LEV):
                keys_here = block[:, lon_step:lon_step + LON, lev_step:lev_step + LEV, :D]
                keys_here = keys_here.reshape(LAT, LON, LEV, HEADS, HEAD_DIM)
                products = lax.optimization_barrier(jnp.sum(query * keys_here, axis=-1))
                lev_fine = (lev_place + lev_step - lev_reach >= 0) & (lev_place + lev_step - lev_reach < LEV)
                allowed = lat_fine[:, None, None, None] & lev_fine[None, None, :, None]
                collected.append(jnp.where(allowed, products, -jnp.inf))
        return (carry, jnp.stack(collected))
    shifts = jnp.arange(WIN_LAT, dtype=jnp.int32)
    _, scores = lax.scan(jax.checkpoint(score_row), None, shifts)
    weights = jax.nn.softmax(scores, axis=(0, 1))

    def mix_row(total, inputs):
        shift, weight_row = inputs
        block = lax.dynamic_slice_in_dim(padded, shift, LAT, 0)
        for lon_step in range(WIN_LON):
            for lev_step in range(WIN_LEV):
                values_here = block[:, lon_step:lon_step + LON, lev_step:lev_step + LEV, D:]
                values_here = values_here.reshape(LAT, LON, LEV, HEADS, HEAD_DIM)
                total = total + weight_row[lon_step * WIN_LEV + lev_step][..., None] * values_here
        return (total, None)
    start = jnp.zeros(query.shape, query.dtype)
    mixed, _ = lax.scan(jax.checkpoint(mix_row), start, (shifts, weights))
    return mixed.reshape(LAT, LON, LEV, D)

def forward(fields, gain, w_qkv, w_out):
    inv_rms = lax.rsqrt(lax.optimization_barrier(jnp.mean(fields * fields, axis=-1, keepdims=True)) + EPSILON)
    normed = fields * inv_rms * gain
    projected = jnp.dot(normed.reshape(-1, D), w_qkv, precision=HIGH).reshape(LAT, LON, LEV, 3 * D)
    query = (projected[..., :D] * HEAD_DIM ** (-0.5)).reshape(LAT, LON, LEV, HEADS, HEAD_DIM)
    mixed = attend(query, projected[..., D:])
    return fields + jnp.dot(mixed.reshape(-1, D), w_out, precision=HIGH).reshape(fields.shape)

def reference(fields, gain, w_qkv, w_out, cotangent):
    output, pullback = jax.vjp(forward, fields, gain, w_qkv, w_out)
    grad_fields, grad_gain, grad_qkv, grad_w_out = pullback(cotangent)
    factor = TOKENS ** (-0.5)
    return (output, grad_fields, grad_gain * factor, grad_qkv * factor, grad_w_out * factor)
```

```python
import jax
import jax.numpy as jnp
import numpy as np
from jax import lax
from jax.experimental import pallas as pl
from jax.experimental.pallas import tpu as pltpu
from jax.sharding import PartitionSpec as P

D = 512
HEADS = 16
HEAD_DIM = 32
LAT_REACH = 3
LON_REACH = 3
LEV_REACH = 1
EPSILON = 1e-06
GROUP = 128
SLAB = 48
TAIL = 64
NEVER = -1e30
F32 = jnp.float32
BF16 = jnp.bfloat16


def split(x):
    high = x.astype(BF16)
    return high, (x - high.astype(F32)).astype(BF16)


def split3(x):
    high = x.astype(BF16)
    rest = x - high.astype(F32)
    middle = rest.astype(BF16)
    return high, middle, (rest - middle.astype(F32)).astype(BF16)


def dot(a, b, ca=1, cb=0):
    return lax.dot_general(a, b, (((ca,), (cb,)), ((), ())), preferred_element_type=F32)


def dot3(a, b, ca=1, cb=0):
    (ah, al), (bh, bl) = a, b
    return dot(ah, bh, ca, cb) + dot(ah, bl, ca, cb) + dot(al, bh, ca, cb)


def dot6(a, b, ca=1, cb=0):
    (ah, am, al), (bh, bm, bl) = a, b
    small = dot(am, bm, ca, cb) + dot(ah, bl, ca, cb) + dot(al, bh, ca, cb)
    return dot(ah, bh, ca, cb) + (dot(ah, bm, ca, cb) + dot(am, bh, ca, cb) + small)


def attention_kernel(
    first, pos_ref, top_ref, mid_ref, bot_ref, gain_ref, wq_ref, wk_ref, wv_ref, wo_ref, cot_ref,
    bias0_ref, bias1_ref, *refs,
):
    if not first:
        out0_ref, bn0_ref, *refs = refs
    if first:
        out_ref, bn_ref, g_ref, *refs = refs
    else:
        out_ref, btop_ref, bmid_ref, bbot_ref, g_ref, *refs = refs
    x_s, n_hi, n_md, n_lo, nt_hi, nt_lo, ot_hi, ot_lo, bn_s, dkv_s, kcat_s, vcat_s, kl_s, vl_s = refs
    step = pl.program_id(0)
    last = pl.num_programs(0) - 1
    rows = x_s.shape[0]
    lats = rows // SLAB
    mid_lats = mid_ref.shape[0]
    tok = mid_lats * 16
    half_tok = tok // 2
    scale = HEAD_DIM ** (-0.5)

    def own_rows(x):
        return x.reshape(lats, SLAB, D)[LAT_REACH:LAT_REACH + mid_lats, :16].reshape(tok, D)

    @pl.when(step == 0)
    def _():
        x = jnp.concatenate([top_ref[...], mid_ref[...], bot_ref[...]], axis=0).reshape(rows, D)
        x_s[...] = x
        inv = lax.rsqrt(jnp.mean(x * x, axis=-1, keepdims=True) + EPSILON)
        normed = x * inv * gain_ref[...]
        n_hi[...], n_md[...], n_lo[...] = split3(normed)
        pad = jnp.zeros((nt_hi.shape[1] - rows, D), F32)
        nt_hi[...], nt_lo[...] = split(jnp.concatenate([normed, pad], axis=0).T)
        ot_hi[...], ot_lo[...] = split(own_rows(normed).T)
        if first:
            bn_s[...] = jnp.zeros(bn_s.shape, F32)
            out_ref[...] = mid_ref[...][:, :16].reshape(tok, D)
        else:
            bn_s[...] = bn0_ref[...].reshape(rows, D)
            out_ref[...] = out0_ref[...]

    wq = split3(wq_ref[...])
    wkv = split3(jnp.concatenate([wk_ref[...], wv_ref[...]], axis=1))
    wo = split3(wo_ref[...])
    normed = (n_hi[...], n_md[...], n_lo[...])
    kv = dot6(normed, wkv)
    k_hi, k_md, k_lo = split3(kv[:, :GROUP])
    v_hi, v_md, v_lo = split3(kv[:, GROUP:])
    kcat_s[:, :GROUP] = k_hi
    kcat_s[:, GROUP:] = k_md
    kl_s[...] = k_lo
    vcat_s[:, :GROUP] = v_hi
    vcat_s[:, GROUP:] = v_md
    vl_s[...] = v_lo
    own_t = (ot_hi[...], ot_lo[...])
    own = tuple(own_rows(x) for x in normed)
    q_t = (dot6(own, wq) * scale).T
    cot = split3(cot_ref[...])
    b_t = dot6(cot, wo, 1, 1).T
    dkv_s[...] = jnp.zeros(dkv_s.shape, F32)
    heads = GROUP // HEAD_DIM
    cols = heads * half_tok
    head_row = lax.broadcasted_iota(jnp.int32, (GROUP, cols), 0) // HEAD_DIM
    head_col = lax.broadcasted_iota(jnp.int32, (GROUP, cols), 1) // half_tok
    same = head_row == head_col
    keys = bias0_ref.shape[1]

    def spread(x):
        return jnp.where(same, jnp.concatenate([x] * heads, axis=1), 0.0)

    def gather(x):
        x = jnp.where(same, x, 0.0)
        y = x[:, :half_tok]
        for h in range(1, heads):
            y = y + x[:, h * half_tok:(h + 1) * half_tok]
        return y

    def against(cat, low, columns):
        hi, md, lo = split3(columns)
        small = dot(jnp.concatenate([cat[:, :GROUP], low], axis=1), jnp.concatenate([lo, hi], axis=0))
        small = small + dot(cat, jnp.concatenate([md, md], axis=0))
        return dot(cat, jnp.concatenate([hi, hi], axis=0)) + small

    mixed_parts, dq_parts = [], []
    for half in range(2):
        lo_row = half * (rows - keys)
        here = slice(lo_row, lo_row + keys)
        kcat = kcat_s[here, :]
        vcat = vcat_s[here, :]
        q_cols = spread(q_t[:, half * half_tok:(half + 1) * half_tok])
        b_cols = spread(b_t[:, half * half_tok:(half + 1) * half_tok])
        bias = (bias0_ref, bias1_ref)[half][0]
        s = against(kcat, kl_s[here, :], q_cols)
        s = s + jnp.concatenate([bias] * (cols // bias.shape[1]), axis=1)
        p = jnp.exp(s - jnp.max(s, axis=0, keepdims=True))
        inv_sum = 1.0 / jnp.sum(p, axis=0, keepdims=True)
        p_hi, p_lo = split(p)
        kcat_t = kcat.T
        vcat_t = vcat.T
        m2 = dot(vcat_t, p_hi)
        mixed_parts.append(gather((m2[:GROUP] + m2[GROUP:] + dot(vcat_t[:GROUP], p_lo)) * inv_sum))
        b_cols = b_cols * inv_sum
        dp = against(vcat, vl_s[here, :], b_cols)
        agreement = jnp.sum(p * dp, axis=0, keepdims=True) * inv_sum
        ds = p * (dp - agreement)
        ds_hi, ds_lo = split(ds)
        dq2 = dot(kcat_t, ds_hi)
        dq_parts.append(gather(dq2[:GROUP] + dq2[GROUP:] + dot(kcat_t[:GROUP], ds_lo)))
        q_rows = split(q_cols.T)
        b_rows = split(b_cols.T)
        dk2 = dot(ds_hi, jnp.concatenate(q_rows, axis=1))
        dk = dk2[:, :GROUP] + dk2[:, GROUP:] + dot(ds_lo, q_rows[0])
        dv2 = dot(p_hi, jnp.concatenate(b_rows, axis=1))
        dv = dv2[:, :GROUP] + dv2[:, GROUP:] + dot(p_lo, b_rows[0])
        dkv_s[here, :GROUP] += dk
        dkv_s[here, GROUP:] += dv
    mixed_t = jnp.concatenate(mixed_parts, axis=1)
    dq = split((jnp.concatenate(dq_parts, axis=1) * scale).T)
    out_ref[...] += dot3(split(mixed_t.T), wo[:2])
    gwo = dot3(split(mixed_t), cot[:2])
    gq = dot3(own_t, dq)
    dkv = split(dkv_s[...])
    gkv = dot3((nt_hi[...], nt_lo[...]), dkv)
    g_ref[0, 0:D, :] = gq
    g_ref[0, D:2 * D, :] = gkv[:, :GROUP]
    g_ref[0, 2 * D:3 * D, :] = gkv[:, GROUP:]
    for j in range(D // GROUP):
        g_ref[0, 3 * D + j * GROUP:3 * D + (j + 1) * GROUP, :] = gwo[:, j * GROUP:(j + 1) * GROUP]
    if not first:
        g_ref[0, 4 * D:, :] = jnp.zeros((TAIL, GROUP), F32)
    bn_s[...] += dot3((dkv[0][:rows], dkv[1][:rows]), wkv[:2], 1, 1)
    back_q = dot3(dq, wq[:2], 1, 1)
    for i in range(mid_lats):
        at = (LAT_REACH + i) * SLAB
        bn_s[at:at + 16, :] += back_q[i * 16:(i + 1) * 16]

    @pl.when(step == last)
    def _():
        bn3 = bn_s[...].reshape(lats, SLAB, D)
        if first:
            bn_ref[...] = bn3
        else:
            btop_ref[...] = bn3[:LAT_REACH]
            bbot_ref[...] = bn3[LAT_REACH + mid_lats:]
            bmid_ref[...] = bn3[LAT_REACH:LAT_REACH + mid_lats]
            x = x_s[...]
            inv = lax.rsqrt(jnp.mean(x * x, axis=-1, keepdims=True) + EPSILON)
            unit = x * inv
            gg = jnp.sum(bn_s[...] * unit, axis=0, keepdims=True)
            for j in range(D // GROUP):
                g_ref[0, 4 * D + j:4 * D + j + 1, :] = gg[:, j * GROUP:(j + 1) * GROUP]


def attention(first, pos, top, mid, bot, gain, w_qkv, w_out, cot, bias, *before):
    mid_lats = mid.shape[0]
    lats = mid_lats + 2 * LAT_REACH
    rows = lats * SLAB
    tok = mid_lats * 16
    padded = -(-rows // 256) * 256
    groups = D // GROUP
    whole = lambda *shape: pl.BlockSpec(shape, lambda s, pos: (0,) * len(shape))
    slab = lambda n: whole(n, SLAB, D)
    like = lambda *shape: jax.ShapeDtypeStruct(shape, F32)
    base = 0 if first else 2
    group = lambda s, pos: base + (1 - pos[0]) * (1 - s) + pos[0] * s
    outs, out_specs = [like(tok, D)], [whole(tok, D)]
    tail = 0 if first else TAIL
    if first:
        outs.append(like(lats, SLAB, D))
        out_specs.append(slab(lats))
    else:
        for n in (LAT_REACH, mid_lats, LAT_REACH):
            outs.append(like(n, SLAB, D))
            out_specs.append(slab(n))
    outs.append(like(2, 4 * D + tail, GROUP))
    out_specs.append(pl.BlockSpec((1, 4 * D + tail, GROUP), lambda s, pos: (s, 0, 0)))
    body = lambda *refs: attention_kernel(first, *refs)
    return pl.pallas_call(
        body,
        grid_spec=pltpu.PrefetchScalarGridSpec(
            num_scalar_prefetch=1,
            grid=(2,),
            in_specs=[
                slab(LAT_REACH), slab(mid_lats), slab(LAT_REACH), whole(1, D),
                pl.BlockSpec((D, GROUP), lambda s, pos: (0, group(s, pos))),
                pl.BlockSpec((D, GROUP), lambda s, pos: (0, groups + group(s, pos))),
                pl.BlockSpec((D, GROUP), lambda s, pos: (0, 2 * groups + group(s, pos))),
                pl.BlockSpec((GROUP, D), lambda s, pos: (group(s, pos), 0)),
                whole(tok, D),
                pl.BlockSpec((1,) + bias.shape[1:], lambda s, pos: (pos[1], 0, 0)),
                pl.BlockSpec((1,) + bias.shape[1:], lambda s, pos: (pos[2], 0, 0)),
            ] + [whole(*x.shape) for x in before],
            out_specs=out_specs,
            scratch_shapes=[
                pltpu.VMEM((rows, D), F32),
                pltpu.VMEM((rows, D), BF16), pltpu.VMEM((rows, D), BF16), pltpu.VMEM((rows, D), BF16),
                pltpu.VMEM((D, padded), BF16), pltpu.VMEM((D, padded), BF16),
                pltpu.VMEM((D, tok), BF16), pltpu.VMEM((D, tok), BF16),
                pltpu.VMEM((rows, D), F32),
                pltpu.VMEM((padded, 2 * GROUP), F32),
                pltpu.VMEM((rows, 2 * GROUP), BF16), pltpu.VMEM((rows, 2 * GROUP), BF16),
                pltpu.VMEM((rows, GROUP), BF16), pltpu.VMEM((rows, GROUP), BF16),
            ],
        ),
        out_shape=outs,
        compiler_params=pltpu.CompilerParams(vmem_limit_bytes=48 * 1024 * 1024),
        cost_estimate=pl.CostEstimate(flops=8_000_000_000, bytes_accessed=16_000_000, transcendentals=1_000_000),
        name="attention",
    )(pos, top, mid, bot, gain.reshape(1, D), w_qkv, w_qkv, w_qkv, w_out, cot, bias, bias, *before)


def unpack_kernel(factor, core_ref, *refs):
    groups = D // GROUP
    *parts, gain_ref, qkv_ref, out_ref = refs
    core = core_ref[0]
    for i, ref in enumerate(parts):
        k, other = divmod(i, 2)
        g = 2 * k + jnp.where(other == 1, 1 - core, core)
        for j in range(3):
            at = pl.multiple_of((j * groups + g) * GROUP, GROUP)
            qkv_ref[:, pl.ds(at, GROUP)] = ref[j * D:(j + 1) * D, :] * factor
        at = pl.multiple_of(g * GROUP, GROUP)
        for j in range(groups):
            out_ref[pl.ds(at, GROUP), j * GROUP:(j + 1) * GROUP] = (
                ref[3 * D + j * GROUP:3 * D + (j + 1) * GROUP, :] * factor
            )
    both = (parts[2][4 * D:4 * D + 8, :] + parts[3][4 * D:4 * D + 8, :]) * factor
    gain_ref[...] = both


def unpack(core, factor, parts):
    return pl.pallas_call(
        lambda *refs: unpack_kernel(factor, *refs),
        in_specs=[pl.BlockSpec(memory_space=pltpu.SMEM)] + [pl.BlockSpec(memory_space=pltpu.VMEM)] * 4,
        out_specs=[pl.BlockSpec(memory_space=pltpu.VMEM)] * 3,
        out_shape=[
            jax.ShapeDtypeStruct((8, GROUP), F32),
            jax.ShapeDtypeStruct((D, 3 * D), F32),
            jax.ShapeDtypeStruct((D, D), F32),
        ],
        compiler_params=pltpu.CompilerParams(vmem_limit_bytes=32 * 1024 * 1024),
        cost_estimate=pl.CostEstimate(flops=1_000_000, bytes_accessed=8_000_000, transcendentals=0),
        name="unpack",
    )(core, *parts)


def shift(x, axis, step, closed):
    count = lax.axis_size(axis)
    ends = count if closed else count - 1
    pairs = [(i, (i + 1) % count) for i in range(ends)]
    if step < 0:
        pairs = [(j, i) for i, j in pairs]
    return lax.ppermute(x, axis, pairs)


def shift_across(x, step):
    count = lax.axis_size("lon")
    pairs = []
    for i in range(count):
        for e in range(2):
            pairs.append((i * 2 + e, ((i + step) % count) * 2 + 1 - e))
    return lax.ppermute(x, ("lon", "lev"), pairs)


def swap_lev(x):
    return lax.ppermute(x, "lev", [(0, 1), (1, 0)])


def window_bias(lat_dev, lon_dev, keys):
    left = np.arange(-LON_REACH, 0)
    right = np.arange(lon_dev, lon_dev + LON_REACH)
    lon = np.concatenate([
        np.repeat(np.arange(lon_dev), 2), np.arange(lon_dev), np.repeat(left, 2), np.repeat(right, 2),
        left, right,
    ])
    level = np.concatenate([
        np.tile([0, 1], lon_dev), np.full(lon_dev, 2), np.tile([0, 1], 2 * LON_REACH),
        np.full(2 * LON_REACH, 2),
    ])
    unused = SLAB - lon.shape[0]
    lon = np.concatenate([lon, np.full(unused, 1000)])
    level = np.concatenate([level, np.full(unused, 0)])
    lats = lat_dev + 2 * LAT_REACH
    rows = lats * SLAB
    lat = np.repeat(np.arange(lats) - LAT_REACH, SLAB)[:, None]
    lon = np.tile(lon, lats)[:, None]
    level = np.tile(level, lats)[:, None]
    q_lat = np.repeat(np.arange(lat_dev), lon_dev * 2)
    q_lon = np.tile(np.repeat(np.arange(lon_dev), 2), lat_dev)
    q_level = np.tile([0, 1], lat_dev * lon_dev)
    near = (np.abs(lat - q_lat) <= LAT_REACH) & (np.abs(lon - q_lon) <= LON_REACH)
    half = q_lat.shape[0] // 2
    table = []
    for part in range(2):
        first = part * (rows - keys)
        ks = slice(first, first + keys)
        qs = np.tile(np.arange(part * half, (part + 1) * half), 2)
        for side in range(2):
            lev_k = np.where(level == 2, 2 - side, side * 2 + level)
            seen = near & (np.abs(lev_k - (side * 2 + q_level)) <= LEV_REACH)
            for edge in range(2):
                kept = seen
                if edge == 1:
                    kept = seen & ((lat >= 0) if part == 0 else (lat < lat_dev))
                table.append(np.where(kept[ks][:, qs], 0.0, NEVER))
    return np.stack(table).astype(np.float32)


def bit_of(axis, bit):
    return (lax.axis_index(axis) >> bit) & 1


def swap_bit(x, axis, bit):
    return lax.ppermute(x, axis, [(i, i ^ (1 << bit)) for i in range(lax.axis_size(axis))])


def halve(blocks, bits):
    sent = []
    for x, (axis, bit) in zip(blocks, bits):
        n = x.shape[0] // 2
        mine = bit_of(axis, bit)
        sent.append(swap_bit(lax.dynamic_slice_in_dim(x, (1 - mine) * n, n, 0), axis, bit))
    kept = []
    for x, s, (axis, bit) in zip(blocks, sent, bits):
        n = x.shape[0] // 2
        kept.append(lax.dynamic_slice_in_dim(x, bit_of(axis, bit) * n, n, 0) + s)
    return kept


def double(blocks, bits):
    came = [swap_bit(x, axis, bit) for x, (axis, bit) in zip(blocks, bits)]
    grown = []
    for x, s, (axis, bit) in zip(blocks, came, bits):
        mine = bit_of(axis, bit) == 1
        grown.append(jnp.concatenate([jnp.where(mine, s, x), jnp.where(mine, x, s)], axis=0))
    return grown


def bits_in(axis):
    count = lax.axis_size(axis)
    assert count & (count - 1) == 0
    return [(axis, b) for b in range(count.bit_length() - 1)]


def exchange_add(blocks, bits):
    came = [swap_bit(x, axis, bit) for x, (axis, bit) in zip(blocks, bits)]
    return [x + y for x, y in zip(blocks, came)]


def after(x, done):
    return lax.optimization_barrier((x, done))[0]


def per_device(fields, gain, w_qkv, w_out, cotangent):
    lat_dev, lon_dev, lev_dev = fields.shape[:3]
    assert lev_dev == 2 and lax.axis_size("lev") == 2 and lon_dev * lev_dev == 16
    tok = lat_dev * lon_dev * lev_dev
    low = lax.axis_index("lev") == 0
    r = LON_REACH
    edge = jnp.where(low, fields[:, :, 1], fields[:, :, 0])
    own = fields.reshape(lat_dev, 16, D)
    left_own = shift(own[:, 16 - 2 * r:], "lon", 1, True)
    right_own = shift(own[:, :2 * r], "lon", -1, True)
    left_far = shift_across(edge[:, lon_dev - r:], 1)
    right_far = shift_across(edge[:, :r], -1)
    far = swap_lev(edge)
    blank = jnp.zeros((lat_dev, SLAB - 24 - 6 * r, D), F32)
    mid = jnp.concatenate([own, far, left_own, right_own, left_far, right_far, blank], axis=1)
    top = shift(mid[lat_dev - LAT_REACH:], "lat", 1, False)
    bot = shift(mid[:LAT_REACH], "lat", -1, False)
    bias = jnp.asarray(window_bias(lat_dev, lon_dev, 512))
    lat_id, lev_id = lax.axis_index("lat"), lax.axis_index("lev")
    core = lat_id & 1
    pos = jnp.stack([
        core, lev_id * 2 + (lat_id == 0), 4 + lev_id * 2 + (lat_id == lax.axis_size("lat") - 1),
    ]).astype(jnp.int32)
    shared = (gain, w_qkv, w_out, cotangent.reshape(tok, D), bias)
    out, bn, g1 = attention(True, pos, top, mid, bot, *shared)
    (pair,), x_bits = bits_in("lat")[:1], bits_in("lat")[1:]
    y_bits, z_bits = bits_in("lev"), bits_in("lon")
    one = g1[1] + swap_bit(g1[0], *pair)
    mid = after(mid, one)
    out, btop, bmid, bbot, g2 = attention(False, pos, top, mid, bot, *shared, out, bn)
    two = g2[1] + swap_bit(g2[0], *pair)
    orders = [
        x_bits + y_bits + z_bits,
        x_bits + y_bits + z_bits,
        z_bits[:-1] + x_bits + y_bits + z_bits[-1:],
    ]
    stages = len(orders[0])
    (one,) = halve([one], [orders[0][0]])
    blocks = [one, two[:2 * D], two[2 * D:]]
    ahead = [1, 0, 0]
    marks = []
    for stage in range(stages - 1):
        live = [i for i in range(3) if stage + ahead[i] < stages - 1]
        new = halve([blocks[i] for i in live], [orders[i][stage + ahead[i]] for i in live])
        for i, x in zip(live, new):
            blocks[i] = x
        marks.append(new[-1])
    blocks = exchange_add(blocks, [order[-1] for order in orders])
    marks.append(blocks[-1])
    for stage in reversed(range(stages - 1)):
        blocks = double(blocks, [order[stage] for order in orders])
        marks.append(blocks[-1])
    one, two = blocks[0], jnp.concatenate(blocks[1:], axis=0)
    one_other, two_other = swap_bit(one, *pair), swap_bit(two, *pair)
    devices = lax.axis_size("lat") * lax.axis_size("lon") * lax.axis_size("lev")
    factor = (tok * devices) ** (-0.5)
    grad_gain, grad_qkv, grad_out = unpack(
        core.reshape(1).astype(jnp.int32), factor, (one, one_other, two, two_other)
    )
    grad_gain = grad_gain[:D // GROUP].reshape(D)
    btop, bbot = after((btop, bbot), marks[0])
    from_low = shift(bbot, "lat", 1, False)
    from_high = shift(btop, "lat", -1, False)
    rest = lat_dev - LAT_REACH
    back = bmid + jnp.pad(from_low, ((0, rest), (0, 0), (0, 0)))
    back = back + jnp.pad(from_high, ((rest, 0), (0, 0), (0, 0)))
    a = 24
    to_left = shift(back[:, a:a + 2 * r], "lon", -1, True)
    to_right = shift(back[:, a + 2 * r:a + 4 * r], "lon", 1, True)
    to_left_far = shift_across(back[:, a + 4 * r:a + 5 * r], -1)
    to_right_far = shift_across(back[:, a + 5 * r:a + 6 * r], 1)
    to_far = swap_lev(back[:, 16:24])
    total = back[:, :16]
    total = total + jnp.pad(to_left, ((0, 0), (16 - 2 * r, 0), (0, 0)))
    total = total + jnp.pad(to_right, ((0, 0), (0, 16 - 2 * r), (0, 0)))
    edge_sum = to_far + jnp.pad(to_left_far, ((0, 0), (lon_dev - r, 0), (0, 0)))
    edge_sum = edge_sum + jnp.pad(to_right_far, ((0, 0), (0, lon_dev - r), (0, 0)))
    at_edge = jnp.where(low, jnp.array([0.0, 1.0]), jnp.array([1.0, 0.0])).astype(F32)
    spread = edge_sum[:, :, None, :] * at_edge[None, None, :, None]
    back_normed = (total + spread.reshape(lat_dev, 16, D)).reshape(tok, D)
    x = fields.reshape(tok, D)
    inv_rms = lax.rsqrt(jnp.mean(x * x, axis=-1, keepdims=True) + EPSILON)
    gain_back = gain * back_normed
    grad_fields = cotangent.reshape(tok, D) + inv_rms * gain_back
    grad_fields = grad_fields - x * inv_rms**3 * jnp.mean(gain_back * x, axis=-1, keepdims=True)
    return (out.reshape(fields.shape), grad_fields.reshape(fields.shape), grad_gain, grad_qkv, grad_out)


def solution(mesh):
    cells = P("lat", "lon", "lev", None)
    return jax.shard_map(
        per_device, mesh=mesh, in_specs=(cells, P(), P(), P(), cells),
        out_specs=(cells, cells, P(), P(), P()), check_vma=False,
    )
```

```python
import jax
import jax.numpy as jnp
import numpy as np
from jax import lax
from jax.experimental import pallas as pl
from jax.experimental.pallas import tpu as pltpu
from jax.sharding import PartitionSpec as P

D = 512
HEADS = 16
HEAD_DIM = 32
LAT_REACH = 3
LON_REACH = 3
LEV_REACH = 1
EPSILON = 1e-06
GROUP = 128
SLAB = 48
TAIL = 64
NEVER = -1e30
F32 = jnp.float32
BF16 = jnp.bfloat16


def split(x):
    high = x.astype(BF16)
    return high, (x - high.astype(F32)).astype(BF16)


def split3(x):
    high = x.astype(BF16)
    rest = x - high.astype(F32)
    middle = rest.astype(BF16)
    return high, middle, (rest - middle.astype(F32)).astype(BF16)


def dot(a, b, ca=1, cb=0):
    return lax.dot_general(a, b, (((ca,), (cb,)), ((), ())), preferred_element_type=F32)


def dot3(a, b, ca=1, cb=0):
    (ah, al), (bh, bl) = a, b
    return dot(ah, bh, ca, cb) + dot(ah, bl, ca, cb) + dot(al, bh, ca, cb)


def left6(parts, axis=1):
    h, m, l = parts
    return jnp.concatenate([h, h, m, m, h, l], axis=axis)


def right6(parts, axis=0):
    h, m, l = parts
    return jnp.concatenate([h, m, h, m, l, h], axis=axis)


def left3(parts, axis=1):
    return jnp.concatenate([parts[0], parts[0], parts[1]], axis=axis)


def right3(parts, axis=0):
    return jnp.concatenate([parts[0], parts[1], parts[0]], axis=axis)


def attention_kernel(
    first, pos_ref, top_ref, mid_ref, bot_ref, gain_ref, wq_ref, wk_ref, wv_ref, wo_ref, cot_ref,
    bias0_ref, bias1_ref, *refs,
):
    if not first:
        out0_ref, bn0_ref, *refs = refs
    if first:
        out_ref, bn_ref, send_ref, keep_ref, *refs = refs
    else:
        out_ref, btop_ref, bmid_ref, bbot_ref, send_ref, keep_ref, *refs = refs
    x_s, n_s, nt_s, own_s, ot_s, c_s, bn_s, dkv_s, k_s, v_s, g_s, sems = refs
    step = pl.program_id(0)
    last = pl.num_programs(0) - 1
    rows = x_s.shape[0]
    lats = rows // SLAB
    mid_lats = mid_ref.shape[0]
    tok = mid_lats * 16
    half_tok = tok // 2
    scale = HEAD_DIM ** (-0.5)
    padded = dkv_s.shape[0]

    def own_rows(x):
        return x.reshape(lats, SLAB, D)[LAT_REACH:LAT_REACH + mid_lats, :16].reshape(tok, D)

    @pl.when(step == 0)
    def _():
        x = jnp.concatenate([top_ref[...], mid_ref[...], bot_ref[...]], axis=0).reshape(rows, D)
        x_s[...] = x
        inv = lax.rsqrt(jnp.mean(x * x, axis=-1, keepdims=True) + EPSILON)
        normed = x * inv * gain_ref[...]
        parts = split3(normed)
        for i, j in enumerate((0, 0, 1, 1, 0, 2)):
            n_s[:, i * D:(i + 1) * D] = parts[j]
            own_s[:, i * D:(i + 1) * D] = own_rows(parts[j])
        pad = jnp.zeros((padded - rows, D), F32)
        parts = split(jnp.concatenate([normed, pad], axis=0).T)
        for i, j in enumerate((0, 0, 1)):
            nt_s[:, i * padded:(i + 1) * padded] = parts[j]
        parts = split(own_rows(normed).T)
        for i, j in enumerate((0, 0, 1)):
            ot_s[:, i * tok:(i + 1) * tok] = parts[j]
        c_s[...] = left6(split3(cot_ref[...]))
        if first:
            bn_s[...] = jnp.zeros(bn_s.shape, F32)
            out_ref[...] = mid_ref[...][:, :16].reshape(tok, D)
        else:
            bn_s[...] = bn0_ref[...].reshape(rows, D)
            out_ref[...] = out0_ref[...]

    wq = split3(wq_ref[...])
    wkv = split3(jnp.concatenate([wk_ref[...], wv_ref[...]], axis=1))
    wo = split3(wo_ref[...])
    kv = dot(n_s[...], right6(wkv))
    k_s[...] = left6(split3(kv[:, :GROUP]))
    v_s[...] = left6(split3(kv[:, GROUP:]))
    q_t = (dot(own_s[...], right6(wq)) * scale).T
    b_t = dot(c_s[...], right6(wo, 1), 1, 1).T
    dkv_s[...] = jnp.zeros(dkv_s.shape, F32)
    heads = GROUP // HEAD_DIM
    cols = heads * half_tok
    head_row = lax.broadcasted_iota(jnp.int32, (GROUP, cols), 0) // HEAD_DIM
    head_col = lax.broadcasted_iota(jnp.int32, (GROUP, cols), 1) // half_tok
    same = head_row == head_col
    keys = bias0_ref.shape[1]

    def spread(x):
        return jnp.where(same, jnp.concatenate([x] * heads, axis=1), 0.0)

    def gather(x):
        x = jnp.where(same, x, 0.0)
        y = x[:, :half_tok]
        for h in range(1, heads):
            y = y + x[:, h * half_tok:(h + 1) * half_tok]
        return y

    mixed_parts, dq_parts = [], []
    for half in range(2):
        lo_row = half * (rows - keys)
        here = slice(lo_row, lo_row + keys)
        q_cols = spread(q_t[:, half * half_tok:(half + 1) * half_tok])
        b_cols = spread(b_t[:, half * half_tok:(half + 1) * half_tok])
        bias = (bias0_ref, bias1_ref)[half][0]
        s = dot(k_s[here, :], right6(split3(q_cols)))
        s = s + jnp.concatenate([bias] * (cols // bias.shape[1]), axis=1)
        p = jnp.exp(s - jnp.max(s, axis=0, keepdims=True))
        inv_sum = 1.0 / jnp.sum(p, axis=0, keepdims=True)
        p_hi, p_lo = split(p)
        kcat_t = k_s[here, GROUP:3 * GROUP].T
        vcat_t = v_s[here, GROUP:3 * GROUP].T
        m2 = dot(vcat_t, p_hi)
        mixed_parts.append(gather((m2[:GROUP] + m2[GROUP:] + dot(vcat_t[:GROUP], p_lo)) * inv_sum))
        b_cols = b_cols * inv_sum
        dp = dot(v_s[here, :], right6(split3(b_cols)))
        agreement = jnp.sum(p * dp, axis=0, keepdims=True) * inv_sum
        ds = p * (dp - agreement)
        ds_hi, ds_lo = split(ds)
        dq2 = dot(kcat_t, ds_hi)
        dq_parts.append(gather(dq2[:GROUP] + dq2[GROUP:] + dot(kcat_t[:GROUP], ds_lo)))
        q_rows = split(q_cols.T)
        b_rows = split(b_cols.T)
        dk2 = dot(ds_hi, jnp.concatenate(q_rows, axis=1))
        dk = dk2[:, :GROUP] + dk2[:, GROUP:] + dot(ds_lo, q_rows[0])
        dv2 = dot(p_hi, jnp.concatenate(b_rows, axis=1))
        dv = dv2[:, :GROUP] + dv2[:, GROUP:] + dot(p_lo, b_rows[0])
        dkv_s[here, :GROUP] += dk
        dkv_s[here, GROUP:] += dv
    mixed_t = jnp.concatenate(mixed_parts, axis=1)
    dq = split((jnp.concatenate(dq_parts, axis=1) * scale).T)
    out_ref[...] += dot(left3(split(mixed_t.T)), right3(wo))
    cot = (c_s[:, :D], c_s[:, 2 * D:3 * D])
    gwo = dot(left3(split(mixed_t)), right3(cot))
    gq = dot(ot_s[...], right3(dq))
    dkv = split(dkv_s[...])
    gkv = dot(nt_s[...], right3(dkv))
    g_s[step, 0:D, :] = gq
    g_s[step, D:2 * D, :] = gkv[:, :GROUP]
    g_s[step, 2 * D:3 * D, :] = gkv[:, GROUP:]
    for j in range(D // GROUP):
        g_s[step, 3 * D + j * GROUP:3 * D + (j + 1) * GROUP, :] = gwo[:, j * GROUP:(j + 1) * GROUP]
    if not first:
        g_s[step, 4 * D:, :] = jnp.zeros((TAIL, GROUP), F32)
    send_copy = pltpu.make_async_copy(g_s.at[0], send_ref, sems.at[0])
    keep_copy = pltpu.make_async_copy(g_s.at[1], keep_ref, sems.at[1])

    @pl.when(step == 0)
    def _():
        send_copy.start()

    bn_s[...] += dot(left3((dkv[0][:rows], dkv[1][:rows])), right3(wkv, 1), 1, 1)
    back_q = dot(left3(dq), right3(wq, 1), 1, 1)
    for i in range(mid_lats):
        at = (LAT_REACH + i) * SLAB
        bn_s[at:at + 16, :] += back_q[i * 16:(i + 1) * 16]

    @pl.when(step == last)
    def _():
        bn3 = bn_s[...].reshape(lats, SLAB, D)
        if first:
            bn_ref[...] = bn3
        else:
            btop_ref[...] = bn3[:LAT_REACH]
            bbot_ref[...] = bn3[LAT_REACH + mid_lats:]
            bmid_ref[...] = bn3[LAT_REACH:LAT_REACH + mid_lats]
            x = x_s[...]
            inv = lax.rsqrt(jnp.mean(x * x, axis=-1, keepdims=True) + EPSILON)
            unit = x * inv
            gg = jnp.sum(bn_s[...] * unit, axis=0, keepdims=True)
            for j in range(D // GROUP):
                g_s[1, 4 * D + j:4 * D + j + 1, :] = gg[:, j * GROUP:(j + 1) * GROUP]
        keep_copy.start()
        send_copy.wait()
        keep_copy.wait()


def attention(first, pos, top, mid, bot, gain, w_qkv, w_out, cot, bias, *before):
    mid_lats = mid.shape[0]
    lats = mid_lats + 2 * LAT_REACH
    rows = lats * SLAB
    tok = mid_lats * 16
    padded = -(-rows // 256) * 256
    groups = D // GROUP
    whole = lambda *shape: pl.BlockSpec(shape, lambda s, pos: (0,) * len(shape))
    slab = lambda n: whole(n, SLAB, D)
    like = lambda *shape: jax.ShapeDtypeStruct(shape, F32)
    base = 0 if first else 2
    group = lambda s, pos: base + (1 - pos[0]) * (1 - s) + pos[0] * s
    outs, out_specs = [like(tok, D)], [whole(tok, D)]
    tail = 0 if first else TAIL
    if first:
        outs.append(like(lats, SLAB, D))
        out_specs.append(slab(lats))
    else:
        for n in (LAT_REACH, mid_lats, LAT_REACH):
            outs.append(like(n, SLAB, D))
            out_specs.append(slab(n))
    for _ in range(2):
        outs.append(like(4 * D + tail, GROUP))
        out_specs.append(pl.BlockSpec(memory_space=pl.ANY))
    body = lambda *refs: attention_kernel(first, *refs)
    return pl.pallas_call(
        body,
        grid_spec=pltpu.PrefetchScalarGridSpec(
            num_scalar_prefetch=1,
            grid=(2,),
            in_specs=[
                slab(LAT_REACH), slab(mid_lats), slab(LAT_REACH), whole(1, D),
                pl.BlockSpec((D, GROUP), lambda s, pos: (0, group(s, pos))),
                pl.BlockSpec((D, GROUP), lambda s, pos: (0, groups + group(s, pos))),
                pl.BlockSpec((D, GROUP), lambda s, pos: (0, 2 * groups + group(s, pos))),
                pl.BlockSpec((GROUP, D), lambda s, pos: (group(s, pos), 0)),
                whole(tok, D),
                pl.BlockSpec((1,) + bias.shape[1:], lambda s, pos: (pos[1], 0, 0)),
                pl.BlockSpec((1,) + bias.shape[1:], lambda s, pos: (pos[2], 0, 0)),
            ] + [whole(*x.shape) for x in before],
            out_specs=out_specs,
            scratch_shapes=[
                pltpu.VMEM((rows, D), F32),
                pltpu.VMEM((rows, 6 * D), BF16), pltpu.VMEM((D, 3 * padded), BF16),
                pltpu.VMEM((tok, 6 * D), BF16), pltpu.VMEM((D, 3 * tok), BF16),
                pltpu.VMEM((tok, 6 * D), BF16),
                pltpu.VMEM((rows, D), F32), pltpu.VMEM((padded, 2 * GROUP), F32),
                pltpu.VMEM((rows, 6 * GROUP), BF16), pltpu.VMEM((rows, 6 * GROUP), BF16),
                pltpu.VMEM((2, 4 * D + tail, GROUP), F32), pltpu.SemaphoreType.DMA((2,)),
            ],
        ),
        out_shape=outs,
        compiler_params=pltpu.CompilerParams(vmem_limit_bytes=48 * 1024 * 1024),
        cost_estimate=pl.CostEstimate(flops=8_000_000_000, bytes_accessed=16_000_000, transcendentals=1_000_000),
        name="attention",
    )(pos, top, mid, bot, gain.reshape(1, D), w_qkv, w_qkv, w_qkv, w_out, cot, bias, bias, *before)


def unpack_kernel(factor, counts, core_ref, mine_ref, other_ref, gain_ref, qkv_ref, out_ref):
    groups = D // GROUP
    core = core_ref[0]
    nz, nx, ny = counts
    count = nz * nx * ny
    rows_a = 2 * D // count
    rows_b = (2 * D + TAIL) // count
    moves = [(0, 0, 0, 4 * D)]
    for i in range(count):
        at = 4 * D + i * (rows_a + rows_b)
        z, x, y = i // (nx * ny), i // ny % nx, i % ny
        moves.append((1, at, ((x * ny + y) * nz + z) * rows_a, rows_a))
        moves.append((1, at + rows_a, 2 * D + i * rows_b, rows_b))
    gain_at = {}
    for ref, keeper in ((mine_ref, core), (other_ref, 1 - core)):
        for k, at, to, size in moves:
            g = 2 * k + keeper
            stop = to + size
            while to < stop:
                tile = to // GROUP
                n = min(stop, (tile + 1) * GROUP) - to
                off = to - tile * GROUP
                j, part = divmod(tile, groups)
                if j < 3:
                    cols = pl.ds(pl.multiple_of((j * groups + g) * GROUP, GROUP), GROUP)
                    row = part * GROUP + off
                    qkv_ref[row:row + n, cols] = ref[at:at + n, :] * factor
                elif j == 3:
                    out_ref[g, off:off + n, part * GROUP:(part + 1) * GROUP] = ref[at:at + n, :] * factor
                else:
                    for row in range(n):
                        gain_at[to - 4 * D + row] = at + row
                to += n
                at += n
    for row in range(D // GROUP):
        at = gain_at[row]
        gain_ref[row:row + 1, :] = (mine_ref[at:at + 1, :] + other_ref[at:at + 1, :]) * factor


def unpack(core, factor, counts, mine, other):
    return pl.pallas_call(
        lambda *refs: unpack_kernel(factor, counts, *refs),
        in_specs=[pl.BlockSpec(memory_space=pltpu.SMEM)] + [pl.BlockSpec(memory_space=pltpu.VMEM)] * 2,
        out_specs=[pl.BlockSpec(memory_space=pltpu.VMEM)] * 3,
        out_shape=[
            jax.ShapeDtypeStruct((D // GROUP, GROUP), F32),
            jax.ShapeDtypeStruct((D, 3 * D), F32),
            jax.ShapeDtypeStruct((D // GROUP, GROUP, D), F32),
        ],
        compiler_params=pltpu.CompilerParams(vmem_limit_bytes=32 * 1024 * 1024),
        cost_estimate=pl.CostEstimate(flops=1_000_000, bytes_accessed=8_000_000, transcendentals=0),
        name="unpack",
    )(core, mine, other)


def shift(x, axis, step, closed):
    count = lax.axis_size(axis)
    ends = count if closed else count - 1
    pairs = [(i, (i + 1) % count) for i in range(ends)]
    if step < 0:
        pairs = [(j, i) for i, j in pairs]
    return lax.ppermute(x, axis, pairs)


def shift_across(x, step):
    count = lax.axis_size("lon")
    pairs = []
    for i in range(count):
        for e in range(2):
            pairs.append((i * 2 + e, ((i + step) % count) * 2 + 1 - e))
    return lax.ppermute(x, ("lon", "lev"), pairs)


def swap_lev(x):
    return lax.ppermute(x, "lev", [(0, 1), (1, 0)])


def window_bias(lat_dev, lon_dev, keys):
    left = np.arange(-LON_REACH, 0)
    right = np.arange(lon_dev, lon_dev + LON_REACH)
    lon = np.concatenate([
        np.repeat(np.arange(lon_dev), 2), np.arange(lon_dev), np.repeat(left, 2), left,
        np.repeat(right, 2), right,
    ])
    level = np.concatenate([
        np.tile([0, 1], lon_dev), np.full(lon_dev, 2), np.tile([0, 1], LON_REACH),
        np.full(LON_REACH, 2), np.tile([0, 1], LON_REACH), np.full(LON_REACH, 2),
    ])
    unused = SLAB - lon.shape[0]
    lon = np.concatenate([lon, np.full(unused, 1000)])
    level = np.concatenate([level, np.full(unused, 0)])
    lats = lat_dev + 2 * LAT_REACH
    rows = lats * SLAB
    lat = np.repeat(np.arange(lats) - LAT_REACH, SLAB)[:, None]
    lon = np.tile(lon, lats)[:, None]
    level = np.tile(level, lats)[:, None]
    q_lat = np.repeat(np.arange(lat_dev), lon_dev * 2)
    q_lon = np.tile(np.repeat(np.arange(lon_dev), 2), lat_dev)
    q_level = np.tile([0, 1], lat_dev * lon_dev)
    near = (np.abs(lat - q_lat) <= LAT_REACH) & (np.abs(lon - q_lon) <= LON_REACH)
    half = q_lat.shape[0] // 2
    table = []
    for part in range(2):
        first = part * (rows - keys)
        ks = slice(first, first + keys)
        qs = np.tile(np.arange(part * half, (part + 1) * half), 2)
        for side in range(2):
            lev_k = np.where(level == 2, 2 - side, side * 2 + level)
            seen = near & (np.abs(lev_k - (side * 2 + q_level)) <= LEV_REACH)
            for edge in range(2):
                kept = seen
                if edge == 1:
                    kept = seen & ((lat >= 0) if part == 0 else (lat < lat_dev))
                table.append(np.where(kept[ks][:, qs], 0.0, NEVER))
    return np.stack(table).astype(np.float32)


def bit_of(axis, bit):
    return (lax.axis_index(axis) >> bit) & 1


def swap_bit(x, axis, bit):
    return lax.ppermute(x, axis, [(i, i ^ (1 << bit)) for i in range(lax.axis_size(axis))])


def halve(blocks, bits):
    def half(block, which):
        terms, start, size = block
        n = size // 2
        return sum(lax.dynamic_slice_in_dim(x, start + which * n, n, 0) for x in terms)

    mine = [bit_of(*bit) for bit in bits]
    given = [half(x, 1 - m) for x, m in zip(blocks, mine)]
    came = [swap_bit(x, *bit) for x, bit in zip(given, bits)]
    if len(came) > 1:
        came = [after(x, given) for x in came]
    kept = [((half(x, m) + s,), 0, s.shape[0]) for x, m, s in zip(blocks, mine, came)]
    return kept, given, came


def double(blocks, bits):
    came = [after(swap_bit(x, *bit), blocks) for x, bit in zip(blocks, bits)]
    grown = []
    for x, s, (axis, bit) in zip(blocks, came, bits):
        mine = bit_of(axis, bit) == 1
        grown.append([jnp.where(mine, s, x), jnp.where(mine, x, s)])
    return grown


def bits_in(axis):
    count = lax.axis_size(axis)
    assert count & (count - 1) == 0
    return [(axis, b) for b in range(count.bit_length() - 1)]


def after(x, done):
    return lax.optimization_barrier((x, done))[0]


def fold(bmid, from_low, from_high, low):
    r = LON_REACH
    lat_dev = bmid.shape[0]
    lon_dev = 8
    rest = lat_dev - LAT_REACH
    back = bmid + jnp.pad(from_low, ((0, rest), (0, 0), (0, 0)))
    back = back + jnp.pad(from_high, ((rest, 0), (0, 0), (0, 0)))
    low_at, high_at = 24, 24 + 3 * r
    to_left = shift(back[:, low_at:high_at], "lon", -1, True)
    to_right = shift(back[:, high_at:high_at + 3 * r], "lon", 1, True)
    total = back[:, :16]
    total = total + jnp.pad(to_left[:, :2 * r], ((0, 0), (16 - 2 * r, 0), (0, 0)))
    total = total + jnp.pad(to_right[:, :2 * r], ((0, 0), (0, 16 - 2 * r), (0, 0)))
    other = back[:, 16:24] + jnp.pad(to_left[:, 2 * r:], ((0, 0), (lon_dev - r, 0), (0, 0)))
    other = other + jnp.pad(to_right[:, 2 * r:], ((0, 0), (0, lon_dev - r), (0, 0)))
    edge_sum = swap_lev(other)
    at_edge = jnp.where(low, jnp.array([0.0, 1.0]), jnp.array([1.0, 0.0])).astype(F32)
    spread = edge_sum[:, :, None, :] * at_edge[None, None, :, None]
    return total + spread.reshape(lat_dev, 16, D), to_left, to_right, edge_sum


def per_device(fields, gain, w_qkv, w_out, cotangent):
    lat_dev, lon_dev, lev_dev = fields.shape[:3]
    assert lev_dev == 2 and lax.axis_size("lev") == 2 and lon_dev * lev_dev == 16
    tok = lat_dev * lon_dev * lev_dev
    low = lax.axis_index("lev") == 0
    r = LON_REACH
    edge = jnp.where(low, fields[:, :, 1], fields[:, :, 0])
    own = fields.reshape(lat_dev, 16, D)
    left_own = shift(own[:, 16 - 2 * r:], "lon", 1, True)
    right_own = shift(own[:, :2 * r], "lon", -1, True)
    left_far = shift_across(edge[:, lon_dev - r:], 1)
    right_far = shift_across(edge[:, :r], -1)
    far = swap_lev(edge)
    blank = jnp.zeros((lat_dev, SLAB - 24 - 6 * r, D), F32)
    mid = jnp.concatenate([own, far, left_own, left_far, right_own, right_far, blank], axis=1)
    top = shift(mid[lat_dev - LAT_REACH:], "lat", 1, False)
    bot = shift(mid[:LAT_REACH], "lat", -1, False)
    bias = jnp.asarray(window_bias(lat_dev, lon_dev, 512))
    lat_id, lev_id = lax.axis_index("lat"), lax.axis_index("lev")
    core = lat_id & 1
    pos = jnp.stack([
        core, lev_id * 2 + (lat_id == 0), 4 + lev_id * 2 + (lat_id == lax.axis_size("lat") - 1),
    ]).astype(jnp.int32)
    shared = (gain, w_qkv, w_out, cotangent.reshape(tok, D), bias)
    out, bn, send, keep = attention(True, pos, top, mid, bot, *shared)
    (pair,), x_bits = bits_in("lat")[:1], bits_in("lat")[1:]
    y_bits, z_bits = bits_in("lev"), bits_in("lon")
    zh_bits = z_bits[:-1]
    orders = [x_bits + y_bits + zh_bits, x_bits + y_bits + zh_bits, zh_bits + x_bits + y_bits]
    stages = len(orders[0])
    (one,), (given,), (came,) = halve([((keep, swap_bit(send, *pair)), 0, 4 * D)], orders[0][:1])
    mid = after(mid, given)
    out, btop, bmid, bbot, send, keep = attention(False, pos, top, mid, bot, *shared, out, bn)
    from_low = shift(bbot, "lat", 1, False)
    from_high = shift(btop, "lat", -1, False)
    two = (keep, swap_bit(after(send, came), *pair))
    blocks = [one, (two, 0, 2 * D), (two, 2 * D, 2 * D + TAIL)]
    for stage in range(stages):
        bits = [order[stage] for order in orders[1:]]
        if stage + 1 < stages:
            blocks, _, _ = halve(blocks, [orders[0][stage + 1]] + bits)
        else:
            blocks[1:], _, _ = halve(blocks[1:], bits)
    size = blocks[0][2]
    every = jnp.concatenate([x[0][0] for x in blocks], axis=0)
    every = every + swap_bit(every, *z_bits[-1])
    every, from_low, from_high = lax.optimization_barrier((every, from_low, from_high))
    back_normed, to_left, to_right, edge_sum = fold(bmid, from_low, from_high, low)
    blocks = [every[:size], every[size:]]
    for stage in reversed(range(stages)):
        if stage == 0:
            blocks[1] = after(blocks[1], (to_left, to_right))
        parts = double(blocks, [orders[0][stage], orders[2][stage]])
        if stage > 0:
            blocks = [jnp.concatenate(x, axis=0) for x in parts]
    mine = after(jnp.concatenate(parts[0] + parts[1], axis=0), edge_sum)
    devices = lax.axis_size("lat") * lax.axis_size("lon") * lax.axis_size("lev")
    factor = (tok * devices) ** (-0.5)
    counts = tuple(1 << len(bits) for bits in (zh_bits, x_bits, y_bits))
    grad_gain, grad_qkv, grad_out = unpack(
        core.reshape(1).astype(jnp.int32), factor, counts,
        mine, swap_bit(mine, *pair),
    )
    grad_gain, grad_out = grad_gain.reshape(D), grad_out.reshape(D, D)
    back_normed = back_normed.reshape(tok, D)
    x = fields.reshape(tok, D)
    inv_rms = lax.rsqrt(jnp.mean(x * x, axis=-1, keepdims=True) + EPSILON)
    gain_back = gain * back_normed
    grad_fields = cotangent.reshape(tok, D) + inv_rms * gain_back
    grad_fields = grad_fields - x * inv_rms**3 * jnp.mean(gain_back * x, axis=-1, keepdims=True)
    return (out.reshape(fields.shape), grad_fields.reshape(fields.shape), grad_gain, grad_qkv, grad_out)


def solution(mesh):
    cells = P("lat", "lon", "lev", None)
    return jax.shard_map(
        per_device, mesh=mesh, in_specs=(cells, P(), P(), P(), cells),
        out_specs=(cells, cells, P(), P(), P()), check_vma=False,
    )
```

```python
import jax
import jax.numpy as jnp
import numpy as np
from jax import lax
from jax.experimental import pallas as pl
from jax.experimental.pallas import tpu as pltpu
from jax.sharding import PartitionSpec as P

D = 512
HEADS = 16
HEAD_DIM = 32
LAT_REACH = 3
LON_REACH = 3
LEV_REACH = 1
EPSILON = 1e-06
GROUP = 128
SLAB = 48
TAIL = 64
NEVER = -1e30
F32 = jnp.float32
BF16 = jnp.bfloat16


def split(x):
    high = x.astype(BF16)
    return high, (x - high.astype(F32)).astype(BF16)


def split3(x):
    high = x.astype(BF16)
    rest = x - high.astype(F32)
    middle = rest.astype(BF16)
    return high, middle, (rest - middle.astype(F32)).astype(BF16)


def dot(a, b, ca=1, cb=0):
    return lax.dot_general(a, b, (((ca,), (cb,)), ((), ())), preferred_element_type=F32)


def dot3(a, b, ca=1, cb=0):
    (ah, al), (bh, bl) = a, b
    return dot(ah, bh, ca, cb) + dot(ah, bl, ca, cb) + dot(al, bh, ca, cb)


def left6(parts, axis=1):
    h, m, l = parts
    return jnp.concatenate([h, h, m, m, h, l], axis=axis)


def right6(parts, axis=0):
    h, m, l = parts
    return jnp.concatenate([h, m, h, m, l, h], axis=axis)


def left3(parts, axis=1):
    return jnp.concatenate([parts[0], parts[0], parts[1]], axis=axis)


def right3(parts, axis=0):
    return jnp.concatenate([parts[0], parts[1], parts[0]], axis=axis)


def attention_kernel(
    pos_ref, top_ref, mid_ref, bot_ref, gain_ref, wq_ref, wk_ref, wv_ref, wo_ref, cot_ref,
    bias0_ref, bias1_ref, out_ref, btop_ref, bmid_ref, bbot_ref, send_ref, keep_ref,
    x_s, n_s, nt_s, own_s, ot_s, c_s, bn_s, dkv_s, k_s, v_s, g_s, t_s, sems,
):
    step = pl.program_id(0)
    last = pl.num_programs(0) - 1
    rows = x_s.shape[0]
    lats = rows // SLAB
    mid_lats = mid_ref.shape[0]
    tok = mid_lats * 16
    half_tok = tok // 2
    scale = HEAD_DIM ** (-0.5)
    padded = dkv_s.shape[0]

    def own_rows(x):
        return x.reshape(lats, SLAB, D)[LAT_REACH:LAT_REACH + mid_lats, :16].reshape(tok, D)

    @pl.when(step == 0)
    def _():
        x = jnp.concatenate([top_ref[...], mid_ref[...], bot_ref[...]], axis=0).reshape(rows, D)
        x_s[...] = x
        inv = lax.rsqrt(jnp.mean(x * x, axis=-1, keepdims=True) + EPSILON)
        normed = x * inv * gain_ref[...]
        parts = split3(normed)
        for i, j in enumerate((0, 0, 1, 1, 0, 2)):
            n_s[:, i * D:(i + 1) * D] = parts[j]
            own_s[:, i * D:(i + 1) * D] = own_rows(parts[j])
        pad = jnp.zeros((padded - rows, D), F32)
        parts = split(jnp.concatenate([normed, pad], axis=0).T)
        for i, j in enumerate((0, 0, 1)):
            nt_s[:, i * padded:(i + 1) * padded] = parts[j]
        parts = split(own_rows(normed).T)
        for i, j in enumerate((0, 0, 1)):
            ot_s[:, i * tok:(i + 1) * tok] = parts[j]
        c_s[...] = left6(split3(cot_ref[...]))
        bn_s[...] = jnp.zeros(bn_s.shape, F32)
        out_ref[...] = mid_ref[...][:, :16].reshape(tok, D)

    wq = split3(wq_ref[...])
    wkv = split3(jnp.concatenate([wk_ref[...], wv_ref[...]], axis=1))
    wo = split3(wo_ref[...])
    kv = dot(n_s[...], right6(wkv))
    k_s[...] = left6(split3(kv[:, :GROUP]))
    v_s[...] = left6(split3(kv[:, GROUP:]))
    q_t = (dot(own_s[...], right6(wq)) * scale).T
    b_t = dot(c_s[...], right6(wo, 1), 1, 1).T
    dkv_s[...] = jnp.zeros(dkv_s.shape, F32)
    heads = GROUP // HEAD_DIM
    cols = heads * half_tok
    head_row = lax.broadcasted_iota(jnp.int32, (GROUP, cols), 0) // HEAD_DIM
    head_col = lax.broadcasted_iota(jnp.int32, (GROUP, cols), 1) // half_tok
    same = head_row == head_col
    keys = bias0_ref.shape[1]

    def spread(x):
        return jnp.where(same, jnp.concatenate([x] * heads, axis=1), 0.0)

    def gather(x):
        x = jnp.where(same, x, 0.0)
        y = x[:, :half_tok]
        for h in range(1, heads):
            y = y + x[:, h * half_tok:(h + 1) * half_tok]
        return y

    halves = range(2)
    here = [slice(h * (rows - keys), h * (rows - keys) + keys) for h in halves]
    q_cols = [spread(q_t[:, h * half_tok:(h + 1) * half_tok]) for h in halves]
    b_cols = [spread(b_t[:, h * half_tok:(h + 1) * half_tok]) for h in halves]
    p, inv_sum, parts, kt, vt = [], [], [], [], []
    for h, bias_ref in enumerate((bias0_ref, bias1_ref)):
        bias = bias_ref[0]
        s = dot(k_s[here[h], :], right6(split3(q_cols[h])))
        s = s + jnp.concatenate([bias] * (cols // bias.shape[1]), axis=1)
        p.append(jnp.exp(s - jnp.max(s, axis=0, keepdims=True)))
        kt.append(k_s[here[h], GROUP:3 * GROUP].T)
        vt.append(v_s[here[h], GROUP:3 * GROUP].T)
    for h in halves:
        inv_sum.append(1.0 / jnp.sum(p[h], axis=0, keepdims=True))
        parts.append(split(p[h]))
        b_cols[h] = b_cols[h] * inv_sum[h]
    mixed_parts, dp = [], []
    for h in halves:
        dp.append(dot(v_s[here[h], :], right6(split3(b_cols[h]))))
        m2 = dot(vt[h], parts[h][0])
        mixed_parts.append(gather((m2[:GROUP] + m2[GROUP:] + dot(vt[h][:GROUP], parts[h][1])) * inv_sum[h]))
    ds = []
    for h in halves:
        agreement = jnp.sum(p[h] * dp[h], axis=0, keepdims=True) * inv_sum[h]
        ds.append(split(p[h] * (dp[h] - agreement)))
        b_rows = split(b_cols[h].T)
        dv2 = dot(parts[h][0], jnp.concatenate(b_rows, axis=1))
        dkv_s[here[h], GROUP:] += dv2[:, :GROUP] + dv2[:, GROUP:] + dot(parts[h][1], b_rows[0])
    dq_parts = []
    for h in halves:
        q_rows = split(q_cols[h].T)
        dk2 = dot(ds[h][0], jnp.concatenate(q_rows, axis=1))
        dkv_s[here[h], :GROUP] += dk2[:, :GROUP] + dk2[:, GROUP:] + dot(ds[h][1], q_rows[0])
        dq2 = dot(kt[h], ds[h][0])
        dq_parts.append(gather(dq2[:GROUP] + dq2[GROUP:] + dot(kt[h][:GROUP], ds[h][1])))
    mixed_t = jnp.concatenate(mixed_parts, axis=1)
    dq = split((jnp.concatenate(dq_parts, axis=1) * scale).T)
    out_ref[...] += dot(left3(split(mixed_t.T)), right3(wo))
    cot = (c_s[:, :D], c_s[:, 2 * D:3 * D])
    gwo = dot(left3(split(mixed_t)), right3(cot))
    gq = dot(ot_s[...], right3(dq))
    dkv = split(dkv_s[...])
    gkv = dot(nt_s[...], right3(dkv))
    copies = [
        pltpu.make_async_copy(
            g_s.at[i % 2], (send_ref, keep_ref)[i // 2].at[pl.ds(i % 2 * 4 * D, 4 * D)], sems.at[i]
        )
        for i in range(4)
    ]
    for i in range(2):
        @pl.when(step == i + 2)
        def _(i=i):
            copies[i].wait()
    slot = step % 2
    g_s[slot, 0:D, :] = gq
    g_s[slot, D:2 * D, :] = gkv[:, :GROUP]
    g_s[slot, 2 * D:3 * D, :] = gkv[:, GROUP:]
    for j in range(D // GROUP):
        g_s[slot, 3 * D + j * GROUP:3 * D + (j + 1) * GROUP, :] = gwo[:, j * GROUP:(j + 1) * GROUP]
    for i in range(4):
        @pl.when(step == i)
        def _(i=i):
            copies[i].start()

    bn_s[...] += dot(left3((dkv[0][:rows], dkv[1][:rows])), right3(wkv, 1), 1, 1)
    back_q = dot(left3(dq), right3(wq, 1), 1, 1)
    for i in range(mid_lats):
        at = (LAT_REACH + i) * SLAB
        bn_s[at:at + 16, :] += back_q[i * 16:(i + 1) * 16]

    @pl.when(step == last)
    def _():
        bn3 = bn_s[...].reshape(lats, SLAB, D)
        btop_ref[...] = bn3[:LAT_REACH]
        bbot_ref[...] = bn3[LAT_REACH + mid_lats:]
        bmid_ref[...] = bn3[LAT_REACH:LAT_REACH + mid_lats]
        x = x_s[...]
        inv = lax.rsqrt(jnp.mean(x * x, axis=-1, keepdims=True) + EPSILON)
        gg = jnp.sum(bn_s[...] * (x * inv), axis=0, keepdims=True)
        t_s[...] = jnp.zeros(t_s.shape, F32)
        for j in range(D // GROUP):
            t_s[1, j:j + 1, :] = gg[:, j * GROUP:(j + 1) * GROUP]
        tails = [
            pltpu.make_async_copy(t_s.at[i], ref.at[pl.ds(8 * D, TAIL)], sems.at[4 + i])
            for i, ref in enumerate((send_ref, keep_ref))
        ]
        for copy in tails:
            copy.start()
        for copy in tails + copies[2:]:
            copy.wait()


def attention(pos, top, mid, bot, gain, w_qkv, w_out, cot, bias):
    mid_lats = mid.shape[0]
    lats = mid_lats + 2 * LAT_REACH
    rows = lats * SLAB
    tok = mid_lats * 16
    padded = -(-rows // 256) * 256
    groups = D // GROUP
    whole = lambda *shape: pl.BlockSpec(shape, lambda s, pos: (0,) * len(shape))
    slab = lambda n: whole(n, SLAB, D)
    like = lambda *shape: jax.ShapeDtypeStruct(shape, F32)
    group = lambda s, pos: 2 * (s % 2) + jnp.where(s < 2, 1 - pos[0], pos[0])
    outs, out_specs = [like(tok, D)], [whole(tok, D)]
    for n in (LAT_REACH, mid_lats, LAT_REACH):
        outs.append(like(n, SLAB, D))
        out_specs.append(slab(n))
    for _ in range(2):
        outs.append(like(8 * D + TAIL, GROUP))
        out_specs.append(pl.BlockSpec(memory_space=pl.ANY))
    return pl.pallas_call(
        attention_kernel,
        grid_spec=pltpu.PrefetchScalarGridSpec(
            num_scalar_prefetch=1,
            grid=(4,),
            in_specs=[
                slab(LAT_REACH), slab(mid_lats), slab(LAT_REACH), whole(1, D),
                pl.BlockSpec((D, GROUP), lambda s, pos: (0, group(s, pos))),
                pl.BlockSpec((D, GROUP), lambda s, pos: (0, groups + group(s, pos))),
                pl.BlockSpec((D, GROUP), lambda s, pos: (0, 2 * groups + group(s, pos))),
                pl.BlockSpec((GROUP, D), lambda s, pos: (group(s, pos), 0)),
                whole(tok, D),
                pl.BlockSpec((1,) + bias.shape[1:], lambda s, pos: (pos[1], 0, 0)),
                pl.BlockSpec((1,) + bias.shape[1:], lambda s, pos: (pos[2], 0, 0)),
            ],
            out_specs=out_specs,
            scratch_shapes=[
                pltpu.VMEM((rows, D), F32),
                pltpu.VMEM((rows, 6 * D), BF16), pltpu.VMEM((D, 3 * padded), BF16),
                pltpu.VMEM((tok, 6 * D), BF16), pltpu.VMEM((D, 3 * tok), BF16),
                pltpu.VMEM((tok, 6 * D), BF16),
                pltpu.VMEM((rows, D), F32), pltpu.VMEM((padded, 2 * GROUP), F32),
                pltpu.VMEM((rows, 6 * GROUP), BF16), pltpu.VMEM((rows, 6 * GROUP), BF16),
                pltpu.VMEM((2, 4 * D, GROUP), F32), pltpu.VMEM((2, TAIL, GROUP), F32),
                pltpu.SemaphoreType.DMA((6,)),
            ],
        ),
        out_shape=outs,
        compiler_params=pltpu.CompilerParams(vmem_limit_bytes=48 * 1024 * 1024),
        cost_estimate=pl.CostEstimate(flops=20_000_000_000, bytes_accessed=24_000_000, transcendentals=2_000_000),
        name="attention",
    )(pos, top, mid, bot, gain.reshape(1, D), w_qkv, w_qkv, w_qkv, w_out, cot, bias, bias)


def unpack_kernel(factor, core_ref, mine_ref, other_ref, gain_ref, qkv_ref, out_ref):
    groups = D // GROUP
    core = core_ref[0]
    for ref, keeper in ((mine_ref, core), (other_ref, 1 - core)):
        for k in range(2):
            g = 2 * k + keeper
            for j in range(3):
                cols = pl.ds(pl.multiple_of((j * groups + g) * GROUP, GROUP), GROUP)
                qkv_ref[:, cols] = ref[(4 * k + j) * D:(4 * k + j + 1) * D, :] * factor
            for j in range(groups):
                at = (4 * k + 3) * D + j * GROUP
                out_ref[g, :, j * GROUP:(j + 1) * GROUP] = ref[at:at + GROUP, :] * factor
    for row in range(D // GROUP):
        at = 8 * D + row
        gain_ref[row:row + 1, :] = (mine_ref[at:at + 1, :] + other_ref[at:at + 1, :]) * factor


def unpack(core, factor, mine, other):
    return pl.pallas_call(
        lambda *refs: unpack_kernel(factor, *refs),
        in_specs=[pl.BlockSpec(memory_space=pltpu.SMEM)] + [pl.BlockSpec(memory_space=pltpu.VMEM)] * 2,
        out_specs=[pl.BlockSpec(memory_space=pltpu.VMEM)] * 3,
        out_shape=[
            jax.ShapeDtypeStruct((D // GROUP, GROUP), F32),
            jax.ShapeDtypeStruct((D, 3 * D), F32),
            jax.ShapeDtypeStruct((D // GROUP, GROUP, D), F32),
        ],
        compiler_params=pltpu.CompilerParams(vmem_limit_bytes=32 * 1024 * 1024),
        cost_estimate=pl.CostEstimate(flops=1_000_000, bytes_accessed=8_000_000, transcendentals=0),
        name="unpack",
    )(core, mine, other)


def shift(x, axis, step, closed):
    count = lax.axis_size(axis)
    ends = count if closed else count - 1
    pairs = [(i, (i + 1) % count) for i in range(ends)]
    if step < 0:
        pairs = [(j, i) for i, j in pairs]
    return lax.ppermute(x, axis, pairs)


def shift_across(x, step):
    count = lax.axis_size("lon")
    pairs = []
    for i in range(count):
        for e in range(2):
            pairs.append((i * 2 + e, ((i + step) % count) * 2 + 1 - e))
    return lax.ppermute(x, ("lon", "lev"), pairs)


def swap_lev(x):
    return lax.ppermute(x, "lev", [(0, 1), (1, 0)])


def window_bias(lat_dev, lon_dev, keys):
    left = np.arange(-LON_REACH, 0)
    right = np.arange(lon_dev, lon_dev + LON_REACH)
    lon = np.concatenate([
        np.repeat(np.arange(lon_dev), 2), np.arange(lon_dev), np.repeat(left, 2), left,
        np.repeat(right, 2), right,
    ])
    level = np.concatenate([
        np.tile([0, 1], lon_dev), np.full(lon_dev, 2), np.tile([0, 1], LON_REACH),
        np.full(LON_REACH, 2), np.tile([0, 1], LON_REACH), np.full(LON_REACH, 2),
    ])
    unused = SLAB - lon.shape[0]
    lon = np.concatenate([lon, np.full(unused, 1000)])
    level = np.concatenate([level, np.full(unused, 0)])
    lats = lat_dev + 2 * LAT_REACH
    rows = lats * SLAB
    lat = np.repeat(np.arange(lats) - LAT_REACH, SLAB)[:, None]
    lon = np.tile(lon, lats)[:, None]
    level = np.tile(level, lats)[:, None]
    q_lat = np.repeat(np.arange(lat_dev), lon_dev * 2)
    q_lon = np.tile(np.repeat(np.arange(lon_dev), 2), lat_dev)
    q_level = np.tile([0, 1], lat_dev * lon_dev)
    near = (np.abs(lat - q_lat) <= LAT_REACH) & (np.abs(lon - q_lon) <= LON_REACH)
    half = q_lat.shape[0] // 2
    table = []
    for part in range(2):
        first = part * (rows - keys)
        ks = slice(first, first + keys)
        qs = np.tile(np.arange(part * half, (part + 1) * half), 2)
        for side in range(2):
            lev_k = np.where(level == 2, 2 - side, side * 2 + level)
            seen = near & (np.abs(lev_k - (side * 2 + q_level)) <= LEV_REACH)
            for edge in range(2):
                kept = seen
                if edge == 1:
                    kept = seen & ((lat >= 0) if part == 0 else (lat < lat_dev))
                table.append(np.where(kept[ks][:, qs], 0.0, NEVER))
    return np.stack(table).astype(np.float32)


def bit_of(axis, bit):
    return (lax.axis_index(axis) >> bit) & 1


def swap_bit(x, axis, bit):
    return lax.ppermute(x, axis, [(i, i ^ (1 << bit)) for i in range(lax.axis_size(axis))])


def halve(blocks, bits):
    def half(block, which):
        terms, start, size = block
        n = size // 2
        return sum(lax.dynamic_slice_in_dim(x, start + which * n, n, 0) for x in terms)

    mine = [bit_of(*bit) for bit in bits]
    given = [half(x, 1 - m) for x, m in zip(blocks, mine)]
    came = [swap_bit(x, *bit) for x, bit in zip(given, bits)]
    if len(came) > 1:
        came = [after(x, given) for x in came]
    kept = [((half(x, m) + s,), 0, s.shape[0]) for x, m, s in zip(blocks, mine, came)]
    return kept


def double(blocks, bits):
    came = [after(swap_bit(x, *bit), blocks) for x, bit in zip(blocks, bits)]
    grown = []
    for x, s, (axis, bit) in zip(blocks, came, bits):
        mine = bit_of(axis, bit) == 1
        grown.append([jnp.where(mine, s, x), jnp.where(mine, x, s)])
    return grown


def bits_in(axis):
    count = lax.axis_size(axis)
    assert count & (count - 1) == 0
    return [(axis, b) for b in range(count.bit_length() - 1)]


def after(x, done):
    return lax.optimization_barrier((x, done))[0]


def finish_kernel(low_ref, back_ref, left_ref, right_ref, edge_ref, x_ref, cot_ref, gain_ref, out_ref):
    r = LON_REACH
    lats, lons = edge_ref.shape[:2]
    low = low_ref[0]
    row = lax.broadcasted_iota(jnp.int32, (2 * lons, lons), 0)
    col = lax.broadcasted_iota(jnp.int32, (2 * lons, lons), 1)
    place = jnp.where(row == 2 * col + low, 1.0, 0.0).astype(F32)
    cells = lax.broadcasted_iota(jnp.int32, (2 * lons, 1), 0)
    gain = gain_ref[...]
    for i in range(lats):
        total = back_ref[i, :16, :]
        none = jnp.zeros((16 - 2 * r, D), F32)
        total = total + jnp.concatenate([none, left_ref[i, :2 * r, :]], axis=0)
        total = total + jnp.concatenate([right_ref[i, :2 * r, :], none], axis=0)
        total = total + jnp.dot(place, edge_ref[i], precision=lax.Precision.HIGHEST, preferred_element_type=F32)
        x = x_ref[i]
        inv_rms = lax.rsqrt(jnp.mean(x * x, axis=-1, keepdims=True) + EPSILON)
        scaled = gain * total
        grad = cot_ref[i * 16:(i + 1) * 16, :] + inv_rms * scaled
        dots = jnp.mean(scaled * x, axis=-1, keepdims=True)
        out_ref[i * 16:(i + 1) * 16, :] = grad - x * (inv_rms * inv_rms * inv_rms * dots)


def finish(low, back, to_left, to_right, edge_sum, own, cot, gain):
    vmem = pl.BlockSpec(memory_space=pltpu.VMEM)
    return pl.pallas_call(
        finish_kernel,
        in_specs=[pl.BlockSpec(memory_space=pltpu.SMEM)] + [vmem] * 7,
        out_specs=vmem,
        out_shape=jax.ShapeDtypeStruct(cot.shape, F32),
        compiler_params=pltpu.CompilerParams(vmem_limit_bytes=16 * 1024 * 1024),
        cost_estimate=pl.CostEstimate(flops=3_000_000, bytes_accessed=3_000_000, transcendentals=0),
        name="finish",
    )(low.astype(jnp.int32).reshape(1), back, to_left, to_right, edge_sum, own, cot, gain.reshape(1, D))


def per_device(fields, gain, w_qkv, w_out, cotangent):
    lat_dev, lon_dev, lev_dev = fields.shape[:3]
    assert lev_dev == 2 and lax.axis_size("lev") == 2 and lon_dev * lev_dev == 16
    tok = lat_dev * lon_dev * lev_dev
    low = lax.axis_index("lev") == 0
    r = LON_REACH
    edge = jnp.where(low, fields[:, :, 1], fields[:, :, 0])
    own = fields.reshape(lat_dev, 16, D)
    left_own = shift(own[:, 16 - 2 * r:], "lon", 1, True)
    right_own = shift(own[:, :2 * r], "lon", -1, True)
    left_far = shift_across(edge[:, lon_dev - r:], 1)
    right_far = shift_across(edge[:, :r], -1)
    far = swap_lev(edge)
    blank = jnp.zeros((lat_dev, SLAB - 24 - 6 * r, D), F32)
    mid = jnp.concatenate([own, far, left_own, left_far, right_own, right_far, blank], axis=1)
    top = shift(mid[lat_dev - LAT_REACH:], "lat", 1, False)
    bot = shift(mid[:LAT_REACH], "lat", -1, False)
    bias = jnp.asarray(window_bias(lat_dev, lon_dev, 512))
    lat_id, lev_id = lax.axis_index("lat"), lax.axis_index("lev")
    core = lat_id & 1
    pos = jnp.stack([
        core, lev_id * 2 + (lat_id == 0), 4 + lev_id * 2 + (lat_id == lax.axis_size("lat") - 1),
    ]).astype(jnp.int32)
    shared = (gain, w_qkv, w_out, cotangent.reshape(tok, D), bias)
    out, btop, bmid, bbot, send, keep = attention(pos, top, mid, bot, *shared)
    from_low = shift(bbot, "lat", 1, False)
    from_high = shift(btop, "lat", -1, False)
    (pair,), x_bits = bits_in("lat")[:1], bits_in("lat")[1:]
    y_bits, z_bits = bits_in("lev"), bits_in("lon")
    zh_bits = z_bits[:-1]
    orders = [x_bits + y_bits + zh_bits, y_bits + zh_bits + x_bits, zh_bits + x_bits + y_bits]
    stages = len(orders[0])
    total = (keep, swap_bit(send, *pair))
    blocks, at, unit = [], 0, (8 * D + TAIL) // TAIL
    for i in range(3):
        size = (unit + 2 - i) // 3 * TAIL
        blocks.append((total, at, size))
        at += size
    rest = lat_dev - LAT_REACH
    low_at, high_at = 24, 24 + 3 * r
    for stage in range(stages):
        blocks = halve(blocks, [order[stage] for order in orders])
        if stage == 0:
            tied = lax.optimization_barrier(([x[0] for x in blocks], from_low, from_high))
            blocks = [(t,) + x[1:] for t, x in zip(tied[0], blocks)]
            back = bmid + jnp.pad(tied[1], ((0, rest), (0, 0), (0, 0)))
            back = back + jnp.pad(tied[2], ((rest, 0), (0, 0), (0, 0)))
            to_left = shift(back[:, low_at:high_at], "lon", -1, True)
            to_right = shift(back[:, high_at:high_at + 3 * r], "lon", 1, True)
    sizes = [x[2] for x in blocks]
    every = jnp.concatenate([x[0][0] for x in blocks], axis=0)
    every, to_left, to_right = lax.optimization_barrier((every, to_left, to_right))
    every = every + swap_bit(every, *z_bits[-1])
    other = back[:, 16:24] + jnp.pad(to_left[:, 2 * r:], ((0, 0), (lon_dev - r, 0), (0, 0)))
    other = other + jnp.pad(to_right[:, 2 * r:], ((0, 0), (0, lon_dev - r), (0, 0)))
    every, edge_sum = lax.optimization_barrier((every, swap_lev(other)))
    grad_fields = finish(
        low, back, to_left, to_right, edge_sum, own, cotangent.reshape(tok, D), gain
    ).reshape(fields.shape)
    blocks = [every[:sizes[0]], every[sizes[0]:sizes[0] + sizes[1]], every[sizes[0] + sizes[1]:]]
    for stage in reversed(range(stages)):
        if stage == 0:
            blocks[0] = after(blocks[0], grad_fields)
        parts = double(blocks, [order[stage] for order in orders])
        if stage > 0:
            blocks = [jnp.concatenate(x, axis=0) for x in parts]
    mine = jnp.concatenate(parts[0] + parts[1] + parts[2], axis=0)
    devices = lax.axis_size("lat") * lax.axis_size("lon") * lax.axis_size("lev")
    factor = (tok * devices) ** (-0.5)
    grad_gain, grad_qkv, grad_out = unpack(
        core.reshape(1).astype(jnp.int32), factor,
        mine, swap_bit(mine, *pair),
    )
    grad_gain, grad_out = grad_gain.reshape(D), grad_out.reshape(D, D)
    return (out.reshape(fields.shape), grad_fields, grad_gain, grad_qkv, grad_out)


def solution(mesh):
    cells = P("lat", "lon", "lev", None)
    return jax.shard_map(
        per_device, mesh=mesh, in_specs=(cells, P(), P(), P(), cells),
        out_specs=(cells, cells, P(), P(), P()), check_vma=False,
    )
```

```python
import jax
import jax.numpy as jnp
import numpy as np
from jax import lax
from jax.experimental import pallas as pl
from jax.experimental.pallas import tpu as pltpu
from jax.sharding import PartitionSpec as P

D = 512
HEADS = 16
HEAD_DIM = 32
LAT_REACH = 3
LON_REACH = 3
LEV_REACH = 1
EPSILON = 1e-06
GROUP = 128
SLAB = 48
TAIL = 64
NEVER = -1e30
F32 = jnp.float32
BF16 = jnp.bfloat16


def split(x):
    high = x.astype(BF16)
    return high, (x - high.astype(F32)).astype(BF16)


def split3(x):
    high = x.astype(BF16)
    rest = x - high.astype(F32)
    middle = rest.astype(BF16)
    return high, middle, (rest - middle.astype(F32)).astype(BF16)


def dot(a, b, ca=1, cb=0):
    return lax.dot_general(a, b, (((ca,), (cb,)), ((), ())), preferred_element_type=F32)


def dot3(a, b, ca=1, cb=0):
    (ah, al), (bh, bl) = a, b
    return dot(ah, bh, ca, cb) + dot(ah, bl, ca, cb) + dot(al, bh, ca, cb)


def left6(parts, axis=1):
    h, m, l = parts
    return jnp.concatenate([h, h, m, m, h, l], axis=axis)


def right6(parts, axis=0):
    h, m, l = parts
    return jnp.concatenate([h, m, h, m, l, h], axis=axis)


def left3(parts, axis=1):
    return jnp.concatenate([parts[0], parts[0], parts[1]], axis=axis)


def right3(parts, axis=0):
    return jnp.concatenate([parts[0], parts[1], parts[0]], axis=axis)


def attention_kernel(
    pos_ref, top_ref, mid_ref, bot_ref, gain_ref, wq_ref, wk_ref, wv_ref, wo_ref, cot_ref,
    bias0_ref, bias1_ref, out_ref, btop_ref, bmid_ref, bbot_ref, send_ref, keep_ref,
    x_s, n_s, nt_s, own_s, ot_s, c_s, bn_s, dkv_s, k_s, v_s, g_s, t_s, sems,
):
    step = pl.program_id(0)
    last = pl.num_programs(0) - 1
    rows = x_s.shape[0]
    lats = rows // SLAB
    mid_lats = mid_ref.shape[0]
    tok = mid_lats * 16
    half_tok = tok // 2
    scale = HEAD_DIM ** (-0.5)
    padded = dkv_s.shape[0]

    def own_rows(x):
        return x.reshape(lats, SLAB, D)[LAT_REACH:LAT_REACH + mid_lats, :16].reshape(tok, D)

    @pl.when(step == 0)
    def _():
        x = jnp.concatenate([top_ref[...], mid_ref[...], bot_ref[...]], axis=0).reshape(rows, D)
        x_s[...] = x
        inv = lax.rsqrt(jnp.mean(x * x, axis=-1, keepdims=True) + EPSILON)
        normed = x * inv * gain_ref[...]
        parts = split3(normed)
        for i, j in enumerate((0, 0, 1, 1, 0, 2)):
            n_s[:, i * D:(i + 1) * D] = parts[j]
            own_s[:, i * D:(i + 1) * D] = own_rows(parts[j])
        pad = jnp.zeros((padded - rows, D), F32)
        parts = split(jnp.concatenate([normed, pad], axis=0).T)
        for i, j in enumerate((0, 0, 1)):
            nt_s[:, i * padded:(i + 1) * padded] = parts[j]
        parts = split(own_rows(normed).T)
        for i, j in enumerate((0, 0, 1)):
            ot_s[:, i * tok:(i + 1) * tok] = parts[j]
        c_s[...] = left6(split3(cot_ref[...]))
        bn_s[...] = jnp.zeros(bn_s.shape, F32)
        out_ref[...] = mid_ref[...][:, :16].reshape(tok, D)

    wq = split3(wq_ref[...])
    wkv = split3(jnp.concatenate([wk_ref[...], wv_ref[...]], axis=1))
    wo = split3(wo_ref[...])
    kv = dot(n_s[...], right6(wkv))
    k_s[...] = left6(split3(kv[:, :GROUP]))
    v_s[...] = left6(split3(kv[:, GROUP:]))
    q_t = (dot(own_s[...], right6(wq)) * scale).T
    b_t = dot(c_s[...], right6(wo, 1), 1, 1).T
    dkv_s[...] = jnp.zeros(dkv_s.shape, F32)
    heads = GROUP // HEAD_DIM
    cols = heads * half_tok
    head_row = lax.broadcasted_iota(jnp.int32, (GROUP, cols), 0) // HEAD_DIM
    head_col = lax.broadcasted_iota(jnp.int32, (GROUP, cols), 1) // half_tok
    same = head_row == head_col
    keys = bias0_ref.shape[1]

    def spread(x):
        return jnp.where(same, jnp.concatenate([x] * heads, axis=1), 0.0)

    def gather(x):
        x = jnp.where(same, x, 0.0)
        y = x[:, :half_tok]
        for h in range(1, heads):
            y = y + x[:, h * half_tok:(h + 1) * half_tok]
        return y

    halves = range(2)
    here = [slice(h * (rows - keys), h * (rows - keys) + keys) for h in halves]
    q_cols = [spread(q_t[:, h * half_tok:(h + 1) * half_tok]) for h in halves]
    b_cols = [spread(b_t[:, h * half_tok:(h + 1) * half_tok]) for h in halves]
    p, inv_sum, parts, kt, vt = [], [], [], [], []
    for h, bias_ref in enumerate((bias0_ref, bias1_ref)):
        bias = bias_ref[0]
        s = dot(k_s[here[h], :], right6(split3(q_cols[h])))
        s = s + jnp.concatenate([bias] * (cols // bias.shape[1]), axis=1)
        p.append(jnp.exp(s - jnp.max(s, axis=0, keepdims=True)))
        kt.append(k_s[here[h], GROUP:3 * GROUP].T)
        vt.append(v_s[here[h], GROUP:3 * GROUP].T)
    for h in halves:
        inv_sum.append(1.0 / jnp.sum(p[h], axis=0, keepdims=True))
        parts.append(split(p[h]))
        b_cols[h] = b_cols[h] * inv_sum[h]
    mixed_parts, dp = [], []
    for h in halves:
        dp.append(dot(v_s[here[h], :], right6(split3(b_cols[h]))))
        m2 = dot(vt[h], parts[h][0])
        mixed_parts.append(gather((m2[:GROUP] + m2[GROUP:] + dot(vt[h][:GROUP], parts[h][1])) * inv_sum[h]))
    ds = []
    for h in halves:
        agreement = jnp.sum(p[h] * dp[h], axis=0, keepdims=True) * inv_sum[h]
        ds.append(split(p[h] * (dp[h] - agreement)))
        b_rows = split(b_cols[h].T)
        dv2 = dot(parts[h][0], jnp.concatenate(b_rows, axis=1))
        dkv_s[here[h], GROUP:] += dv2[:, :GROUP] + dv2[:, GROUP:] + dot(parts[h][1], b_rows[0])
    dq_parts = []
    for h in halves:
        q_rows = split(q_cols[h].T)
        dk2 = dot(ds[h][0], jnp.concatenate(q_rows, axis=1))
        dkv_s[here[h], :GROUP] += dk2[:, :GROUP] + dk2[:, GROUP:] + dot(ds[h][1], q_rows[0])
        dq2 = dot(kt[h], ds[h][0])
        dq_parts.append(gather(dq2[:GROUP] + dq2[GROUP:] + dot(kt[h][:GROUP], ds[h][1])))
    mixed_t = jnp.concatenate(mixed_parts, axis=1)
    dq = split((jnp.concatenate(dq_parts, axis=1) * scale).T)
    out_ref[...] += dot(left3(split(mixed_t.T)), right3(wo))
    cot = (c_s[:, :D], c_s[:, 2 * D:3 * D])
    gwo = dot(left3(split(mixed_t)), right3(cot))
    gq = dot(ot_s[...], right3(dq))
    dkv = split(dkv_s[...])
    gkv = dot(nt_s[...], right3(dkv))
    copies = [
        pltpu.make_async_copy(
            g_s.at[i % 2], (send_ref, keep_ref)[i // 2].at[pl.ds(i % 2 * 4 * D, 4 * D)], sems.at[i]
        )
        for i in range(4)
    ]
    for i in range(2):
        @pl.when(step == i + 2)
        def _(i=i):
            copies[i].wait()
    slot = step % 2
    g_s[slot, 0:D, :] = gq
    g_s[slot, D:2 * D, :] = gkv[:, :GROUP]
    g_s[slot, 2 * D:3 * D, :] = gkv[:, GROUP:]
    for j in range(D // GROUP):
        g_s[slot, 3 * D + j * GROUP:3 * D + (j + 1) * GROUP, :] = gwo[:, j * GROUP:(j + 1) * GROUP]
    for i in range(4):
        @pl.when(step == i)
        def _(i=i):
            copies[i].start()

    bn_s[...] += dot(left3((dkv[0][:rows], dkv[1][:rows])), right3(wkv, 1), 1, 1)
    back_q = dot(left3(dq), right3(wq, 1), 1, 1)
    for i in range(mid_lats):
        at = (LAT_REACH + i) * SLAB
        bn_s[at:at + 16, :] += back_q[i * 16:(i + 1) * 16]

    @pl.when(step == last)
    def _():
        bn3 = bn_s[...].reshape(lats, SLAB, D)
        btop_ref[...] = bn3[:LAT_REACH]
        bbot_ref[...] = bn3[LAT_REACH + mid_lats:]
        bmid_ref[...] = bn3[LAT_REACH:LAT_REACH + mid_lats]
        x = x_s[...]
        inv = lax.rsqrt(jnp.mean(x * x, axis=-1, keepdims=True) + EPSILON)
        gg = jnp.sum(bn_s[...] * (x * inv), axis=0, keepdims=True)
        t_s[...] = jnp.zeros(t_s.shape, F32)
        for j in range(D // GROUP):
            t_s[1, j:j + 1, :] = gg[:, j * GROUP:(j + 1) * GROUP]
        tails = [
            pltpu.make_async_copy(t_s.at[i], ref.at[pl.ds(8 * D, TAIL)], sems.at[4 + i])
            for i, ref in enumerate((send_ref, keep_ref))
        ]
        for copy in tails:
            copy.start()
        for copy in tails + copies[2:]:
            copy.wait()


def attention(pos, top, mid, bot, gain, w_qkv, w_out, cot, bias):
    mid_lats = mid.shape[0]
    lats = mid_lats + 2 * LAT_REACH
    rows = lats * SLAB
    tok = mid_lats * 16
    padded = -(-rows // 256) * 256
    groups = D // GROUP
    whole = lambda *shape: pl.BlockSpec(shape, lambda s, pos: (0,) * len(shape))
    slab = lambda n: whole(n, SLAB, D)
    like = lambda *shape: jax.ShapeDtypeStruct(shape, F32)
    group = lambda s, pos: 2 * (s % 2) + jnp.where(s < 2, 1 - pos[0], pos[0])
    outs, out_specs = [like(tok, D)], [whole(tok, D)]
    for n in (LAT_REACH, mid_lats, LAT_REACH):
        outs.append(like(n, SLAB, D))
        out_specs.append(slab(n))
    for _ in range(2):
        outs.append(like(8 * D + TAIL, GROUP))
        out_specs.append(pl.BlockSpec(memory_space=pl.ANY))
    return pl.pallas_call(
        attention_kernel,
        grid_spec=pltpu.PrefetchScalarGridSpec(
            num_scalar_prefetch=1,
            grid=(4,),
            in_specs=[
                slab(LAT_REACH), slab(mid_lats), slab(LAT_REACH), whole(1, D),
                pl.BlockSpec((D, GROUP), lambda s, pos: (0, group(s, pos))),
                pl.BlockSpec((D, GROUP), lambda s, pos: (0, groups + group(s, pos))),
                pl.BlockSpec((D, GROUP), lambda s, pos: (0, 2 * groups + group(s, pos))),
                pl.BlockSpec((GROUP, D), lambda s, pos: (group(s, pos), 0)),
                whole(tok, D),
                pl.BlockSpec((1,) + bias.shape[1:], lambda s, pos: (pos[1], 0, 0)),
                pl.BlockSpec((1,) + bias.shape[1:], lambda s, pos: (pos[2], 0, 0)),
            ],
            out_specs=out_specs,
            scratch_shapes=[
                pltpu.VMEM((rows, D), F32),
                pltpu.VMEM((rows, 6 * D), BF16), pltpu.VMEM((D, 3 * padded), BF16),
                pltpu.VMEM((tok, 6 * D), BF16), pltpu.VMEM((D, 3 * tok), BF16),
                pltpu.VMEM((tok, 6 * D), BF16),
                pltpu.VMEM((rows, D), F32), pltpu.VMEM((padded, 2 * GROUP), F32),
                pltpu.VMEM((rows, 6 * GROUP), BF16), pltpu.VMEM((rows, 6 * GROUP), BF16),
                pltpu.VMEM((2, 4 * D, GROUP), F32), pltpu.VMEM((2, TAIL, GROUP), F32),
                pltpu.SemaphoreType.DMA((6,)),
            ],
        ),
        out_shape=outs,
        compiler_params=pltpu.CompilerParams(vmem_limit_bytes=54 * 1024 * 1024),
        cost_estimate=pl.CostEstimate(flops=20_000_000_000, bytes_accessed=24_000_000, transcendentals=2_000_000),
        name="attention",
    )(pos, top, mid, bot, gain.reshape(1, D), w_qkv, w_qkv, w_qkv, w_out, cot, bias, bias)


def unpack_kernel(factor, core_ref, mine_ref, other_ref, gain_ref, qkv_ref, out_ref):
    groups = D // GROUP
    core = core_ref[0]
    for ref, keeper in ((mine_ref, core), (other_ref, 1 - core)):
        for k in range(2):
            g = 2 * k + keeper
            for j in range(3):
                cols = pl.ds(pl.multiple_of((j * groups + g) * GROUP, GROUP), GROUP)
                qkv_ref[:, cols] = ref[(4 * k + j) * D:(4 * k + j + 1) * D, :] * factor
            for j in range(groups):
                at = (4 * k + 3) * D + j * GROUP
                out_ref[g, :, j * GROUP:(j + 1) * GROUP] = ref[at:at + GROUP, :] * factor
    for row in range(D // GROUP):
        at = 8 * D + row
        gain_ref[row:row + 1, :] = (mine_ref[at:at + 1, :] + other_ref[at:at + 1, :]) * factor


def unpack(core, factor, mine, other):
    return pl.pallas_call(
        lambda *refs: unpack_kernel(factor, *refs),
        in_specs=[pl.BlockSpec(memory_space=pltpu.SMEM)] + [pl.BlockSpec(memory_space=pltpu.VMEM)] * 2,
        out_specs=[pl.BlockSpec(memory_space=pltpu.VMEM)] * 3,
        out_shape=[
            jax.ShapeDtypeStruct((D // GROUP, GROUP), F32),
            jax.ShapeDtypeStruct((D, 3 * D), F32),
            jax.ShapeDtypeStruct((D // GROUP, GROUP, D), F32),
        ],
        compiler_params=pltpu.CompilerParams(vmem_limit_bytes=32 * 1024 * 1024),
        cost_estimate=pl.CostEstimate(flops=1_000_000, bytes_accessed=8_000_000, transcendentals=0),
        name="unpack",
    )(core, mine, other)


def shift(x, axis, step, closed):
    count = lax.axis_size(axis)
    ends = count if closed else count - 1
    pairs = [(i, (i + 1) % count) for i in range(ends)]
    if step < 0:
        pairs = [(j, i) for i, j in pairs]
    return lax.ppermute(x, axis, pairs)


def shift_across(x, step):
    count = lax.axis_size("lon")
    pairs = []
    for i in range(count):
        for e in range(2):
            pairs.append((i * 2 + e, ((i + step) % count) * 2 + 1 - e))
    return lax.ppermute(x, ("lon", "lev"), pairs)


def swap_lev(x):
    return lax.ppermute(x, "lev", [(0, 1), (1, 0)])


def window_bias(lat_dev, lon_dev, keys):
    left = np.arange(-LON_REACH, 0)
    right = np.arange(lon_dev, lon_dev + LON_REACH)
    lon = np.concatenate([
        np.repeat(np.arange(lon_dev), 2), np.arange(lon_dev), np.repeat(left, 2), left,
        np.repeat(right, 2), right,
    ])
    level = np.concatenate([
        np.tile([0, 1], lon_dev), np.full(lon_dev, 2), np.tile([0, 1], LON_REACH),
        np.full(LON_REACH, 2), np.tile([0, 1], LON_REACH), np.full(LON_REACH, 2),
    ])
    unused = SLAB - lon.shape[0]
    lon = np.concatenate([lon, np.full(unused, 1000)])
    level = np.concatenate([level, np.full(unused, 0)])
    lats = lat_dev + 2 * LAT_REACH
    rows = lats * SLAB
    lat = np.repeat(np.arange(lats) - LAT_REACH, SLAB)[:, None]
    lon = np.tile(lon, lats)[:, None]
    level = np.tile(level, lats)[:, None]
    q_lat = np.repeat(np.arange(lat_dev), lon_dev * 2)
    q_lon = np.tile(np.repeat(np.arange(lon_dev), 2), lat_dev)
    q_level = np.tile([0, 1], lat_dev * lon_dev)
    near = (np.abs(lat - q_lat) <= LAT_REACH) & (np.abs(lon - q_lon) <= LON_REACH)
    half = q_lat.shape[0] // 2
    table = []
    for part in range(2):
        first = part * (rows - keys)
        ks = slice(first, first + keys)
        qs = np.tile(np.arange(part * half, (part + 1) * half), 2)
        for side in range(2):
            lev_k = np.where(level == 2, 2 - side, side * 2 + level)
            seen = near & (np.abs(lev_k - (side * 2 + q_level)) <= LEV_REACH)
            for edge in range(2):
                kept = seen
                if edge == 1:
                    kept = seen & ((lat >= 0) if part == 0 else (lat < lat_dev))
                table.append(np.where(kept[ks][:, qs], 0.0, NEVER))
    return np.stack(table).astype(np.float32)


def bit_of(axis, bit):
    return (lax.axis_index(axis) >> bit) & 1


def swap_bit(x, axis, bit):
    return lax.ppermute(x, axis, [(i, i ^ (1 << bit)) for i in range(lax.axis_size(axis))])


def halve(blocks, bits):
    def half(block, which):
        terms, start, size = block
        n = size // 2
        return sum(lax.dynamic_slice_in_dim(x, start + which * n, n, 0) for x in terms)

    mine = [bit_of(*bit) for bit in bits]
    given = [half(x, 1 - m) for x, m in zip(blocks, mine)]
    came = [swap_bit(x, *bit) for x, bit in zip(given, bits)]
    if len(came) > 1:
        came = [after(x, given) for x in came]
    kept = [((half(x, m) + s,), 0, s.shape[0]) for x, m, s in zip(blocks, mine, came)]
    return kept


def double(blocks, bits):
    came = [after(swap_bit(x, *bit), blocks) for x, bit in zip(blocks, bits)]
    grown = []
    for x, s, (axis, bit) in zip(blocks, came, bits):
        mine = bit_of(axis, bit) == 1
        grown.append([jnp.where(mine, s, x), jnp.where(mine, x, s)])
    return grown


def bits_in(axis):
    count = lax.axis_size(axis)
    assert count & (count - 1) == 0
    return [(axis, b) for b in range(count.bit_length() - 1)]


def after(x, done):
    return lax.optimization_barrier((x, done))[0]


def finish_kernel(low_ref, back_ref, left_ref, right_ref, edge_ref, x_ref, cot_ref, gain_ref, out_ref):
    r = LON_REACH
    lats, lons = edge_ref.shape[:2]
    low = low_ref[0]
    row = lax.broadcasted_iota(jnp.int32, (2 * lons, lons), 0)
    col = lax.broadcasted_iota(jnp.int32, (2 * lons, lons), 1)
    place = jnp.where(row == 2 * col + low, 1.0, 0.0).astype(F32)
    cells = lax.broadcasted_iota(jnp.int32, (2 * lons, 1), 0)
    gain = gain_ref[...]
    for i in range(lats):
        total = back_ref[i, :16, :]
        none = jnp.zeros((16 - 2 * r, D), F32)
        total = total + jnp.concatenate([none, left_ref[i, :2 * r, :]], axis=0)
        total = total + jnp.concatenate([right_ref[i, :2 * r, :], none], axis=0)
        total = total + jnp.dot(place, edge_ref[i], precision=lax.Precision.HIGHEST, preferred_element_type=F32)
        x = x_ref[i]
        inv_rms = lax.rsqrt(jnp.mean(x * x, axis=-1, keepdims=True) + EPSILON)
        scaled = gain * total
        grad = cot_ref[i * 16:(i + 1) * 16, :] + inv_rms * scaled
        dots = jnp.mean(scaled * x, axis=-1, keepdims=True)
        out_ref[i * 16:(i + 1) * 16, :] = grad - x * (inv_rms * inv_rms * inv_rms * dots)


def finish(low, back, to_left, to_right, edge_sum, own, cot, gain):
    vmem = pl.BlockSpec(memory_space=pltpu.VMEM)
    return pl.pallas_call(
        finish_kernel,
        in_specs=[pl.BlockSpec(memory_space=pltpu.SMEM)] + [vmem] * 7,
        out_specs=vmem,
        out_shape=jax.ShapeDtypeStruct(cot.shape, F32),
        compiler_params=pltpu.CompilerParams(vmem_limit_bytes=16 * 1024 * 1024),
        cost_estimate=pl.CostEstimate(flops=3_000_000, bytes_accessed=3_000_000, transcendentals=0),
        name="finish",
    )(low.astype(jnp.int32).reshape(1), back, to_left, to_right, edge_sum, own, cot, gain.reshape(1, D))


def per_device(fields, gain, w_qkv, w_out, cotangent):
    lat_dev, lon_dev, lev_dev = fields.shape[:3]
    assert lev_dev == 2 and lax.axis_size("lev") == 2 and lon_dev * lev_dev == 16
    tok = lat_dev * lon_dev * lev_dev
    low = lax.axis_index("lev") == 0
    r = LON_REACH
    edge = jnp.where(low, fields[:, :, 1], fields[:, :, 0])
    own = fields.reshape(lat_dev, 16, D)
    left_own = shift(own[:, 16 - 2 * r:], "lon", 1, True)
    right_own = shift(own[:, :2 * r], "lon", -1, True)
    left_far = shift_across(edge[:, lon_dev - r:], 1)
    right_far = shift_across(edge[:, :r], -1)
    far = swap_lev(edge)
    blank = jnp.zeros((lat_dev, SLAB - 24 - 6 * r, D), F32)
    mid = jnp.concatenate([own, far, left_own, left_far, right_own, right_far, blank], axis=1)
    top = shift(mid[lat_dev - LAT_REACH:], "lat", 1, False)
    bot = shift(mid[:LAT_REACH], "lat", -1, False)
    bias = jnp.asarray(window_bias(lat_dev, lon_dev, 512))
    lat_id, lev_id = lax.axis_index("lat"), lax.axis_index("lev")
    core = lat_id & 1
    pos = jnp.stack([
        core, lev_id * 2 + (lat_id == 0), 4 + lev_id * 2 + (lat_id == lax.axis_size("lat") - 1),
    ]).astype(jnp.int32)
    shared = (gain, w_qkv, w_out, cotangent.reshape(tok, D), bias)
    out, btop, bmid, bbot, send, keep = attention(pos, top, mid, bot, *shared)
    from_low = shift(bbot, "lat", 1, False)
    from_high = shift(btop, "lat", -1, False)
    (pair,), x_bits = bits_in("lat")[:1], bits_in("lat")[1:]
    y_bits, z_bits = bits_in("lev"), bits_in("lon")
    zh_bits = z_bits[:-1]
    orders = [x_bits + y_bits + zh_bits, y_bits + zh_bits + x_bits, zh_bits + x_bits + y_bits]
    stages = len(orders[0])
    total = (keep, swap_bit(send, *pair))
    blocks, at, unit = [], 0, (8 * D + TAIL) // TAIL
    for i in range(3):
        size = (unit + 2 - i) // 3 * TAIL
        blocks.append((total, at, size))
        at += size
    rest = lat_dev - LAT_REACH
    low_at, high_at = 24, 24 + 3 * r
    for stage in range(stages):
        blocks = halve(blocks, [order[stage] for order in orders])
        if stage == 0:
            tied = lax.optimization_barrier(([x[0] for x in blocks], from_low, from_high))
            blocks = [(t,) + x[1:] for t, x in zip(tied[0], blocks)]
            back = bmid + jnp.pad(tied[1], ((0, rest), (0, 0), (0, 0)))
            back = back + jnp.pad(tied[2], ((rest, 0), (0, 0), (0, 0)))
            to_left = shift(back[:, low_at:high_at], "lon", -1, True)
            to_right = shift(back[:, high_at:high_at + 3 * r], "lon", 1, True)
    sizes = [x[2] for x in blocks]
    every = jnp.concatenate([x[0][0] for x in blocks], axis=0)
    every, to_left, to_right = lax.optimization_barrier((every, to_left, to_right))
    every = every + swap_bit(every, *z_bits[-1])
    other = back[:, 16:24] + jnp.pad(to_left[:, 2 * r:], ((0, 0), (lon_dev - r, 0), (0, 0)))
    other = other + jnp.pad(to_right[:, 2 * r:], ((0, 0), (0, lon_dev - r), (0, 0)))
    every, edge_sum = lax.optimization_barrier((every, swap_lev(other)))
    grad_fields = finish(
        low, back, to_left, to_right, edge_sum, own, cotangent.reshape(tok, D), gain
    ).reshape(fields.shape)
    blocks = [every[:sizes[0]], every[sizes[0]:sizes[0] + sizes[1]], every[sizes[0] + sizes[1]:]]
    for stage in reversed(range(stages)):
        if stage == 0:
            blocks[0] = after(blocks[0], grad_fields)
        parts = double(blocks, [order[stage] for order in orders])
        if stage > 0:
            blocks = [jnp.concatenate(x, axis=0) for x in parts]
    mine = jnp.concatenate(parts[0] + parts[1] + parts[2], axis=0)
    devices = lax.axis_size("lat") * lax.axis_size("lon") * lax.axis_size("lev")
    factor = (tok * devices) ** (-0.5)
    grad_gain, grad_qkv, grad_out = unpack(
        core.reshape(1).astype(jnp.int32), factor,
        mine, swap_bit(mine, *pair),
    )
    grad_gain, grad_out = grad_gain.reshape(D), grad_out.reshape(D, D)
    return (out.reshape(fields.shape), grad_fields, grad_gain, grad_qkv, grad_out)


def solution(mesh):
    cells = P("lat", "lon", "lev", None)
    return jax.shard_map(
        per_device, mesh=mesh, in_specs=(cells, P(), P(), P(), cells),
        out_specs=(cells, cells, P(), P(), P()), check_vma=False,
    )
```

```python
import jax
import jax.numpy as jnp
import numpy as np
from jax import lax
from jax.experimental import pallas as pl
from jax.experimental.pallas import tpu as pltpu
from jax.sharding import PartitionSpec as P

D = 512
HEADS = 16
HEAD_DIM = 32
LAT_REACH = 3
LON_REACH = 3
LEV_REACH = 1
EPSILON = 1e-06
GROUP = 128
SLAB = 48
TAIL = 64
NEVER = -1e30
F32 = jnp.float32
BF16 = jnp.bfloat16


def split(x):
    high = x.astype(BF16)
    return high, (x - high.astype(F32)).astype(BF16)


def split3(x):
    high = x.astype(BF16)
    rest = x - high.astype(F32)
    middle = rest.astype(BF16)
    return high, middle, (rest - middle.astype(F32)).astype(BF16)


def dot(a, b, ca=1, cb=0):
    return lax.dot_general(a, b, (((ca,), (cb,)), ((), ())), preferred_element_type=F32)


def dot3(a, b, ca=1, cb=0):
    (ah, al), (bh, bl) = a, b
    return dot(ah, bh, ca, cb) + dot(ah, bl, ca, cb) + dot(al, bh, ca, cb)


def left6(parts, axis=1):
    h, m, l = parts
    return jnp.concatenate([h, h, m, m, h, l], axis=axis)


def right6(parts, axis=0):
    h, m, l = parts
    return jnp.concatenate([h, m, h, m, l, h], axis=axis)


def left3(parts, axis=1):
    return jnp.concatenate([parts[0], parts[0], parts[1]], axis=axis)


def right3(parts, axis=0):
    return jnp.concatenate([parts[0], parts[1], parts[0]], axis=axis)


def attention_kernel(
    pos_ref, top_ref, mid_ref, bot_ref, gain_ref, wq_ref, wk_ref, wv_ref, wo_ref, cot_ref,
    bias0_ref, bias1_ref, out_ref, btop_ref, bmid_ref, bbot_ref, send_ref, keep_ref,
    x_s, n_s, nt_s, own_s, ot_s, c_s, bn_s, dkv_s, k_s, v_s, g_s, t_s, sems,
):
    step = pl.program_id(0)
    last = pl.num_programs(0) - 1
    rows = x_s.shape[0]
    lats = rows // SLAB
    mid_lats = mid_ref.shape[0]
    tok = mid_lats * 16
    half_tok = tok // 2
    scale = HEAD_DIM ** (-0.5)
    padded = dkv_s.shape[0]

    def own_rows(x):
        return x.reshape(lats, SLAB, D)[LAT_REACH:LAT_REACH + mid_lats, :16].reshape(tok, D)

    @pl.when(step == 0)
    def _():
        x = jnp.concatenate([top_ref[...], mid_ref[...], bot_ref[...]], axis=0).reshape(rows, D)
        x_s[...] = x
        inv = lax.rsqrt(jnp.mean(x * x, axis=-1, keepdims=True) + EPSILON)
        normed = x * inv * gain_ref[...]
        parts = split3(normed)
        for i, j in enumerate((0, 0, 1, 1, 0, 2)):
            n_s[:, i * D:(i + 1) * D] = parts[j]
            own_s[:, i * D:(i + 1) * D] = own_rows(parts[j])
        pad = jnp.zeros((padded - rows, D), F32)
        parts = split(jnp.concatenate([normed, pad], axis=0).T)
        for i, j in enumerate((0, 0, 1)):
            nt_s[:, i * padded:(i + 1) * padded] = parts[j]
        parts = split(own_rows(normed).T)
        for i, j in enumerate((0, 0, 1)):
            ot_s[:, i * tok:(i + 1) * tok] = parts[j]
        c_s[...] = left6(split3(cot_ref[...]))
        bn_s[...] = jnp.zeros(bn_s.shape, F32)
        out_ref[...] = mid_ref[...][:, :16].reshape(tok, D)

    wq = split3(wq_ref[...])
    wkv = split3(jnp.concatenate([wk_ref[...], wv_ref[...]], axis=1))
    wo = split3(wo_ref[...])
    kv = dot(n_s[...], right6(wkv))
    k_s[...] = left6(split3(kv[:, :GROUP]))
    v_s[...] = left6(split3(kv[:, GROUP:]))
    q_t = (dot(own_s[...], right6(wq)) * scale).T
    b_t = dot(c_s[...], right6(wo, 1), 1, 1).T
    dkv_s[...] = jnp.zeros(dkv_s.shape, F32)
    heads = GROUP // HEAD_DIM
    cols = heads * half_tok
    head_row = lax.broadcasted_iota(jnp.int32, (GROUP, cols), 0) // HEAD_DIM
    head_col = lax.broadcasted_iota(jnp.int32, (GROUP, cols), 1) // half_tok
    same = head_row == head_col
    keys = bias0_ref.shape[1]

    def spread(x):
        return jnp.where(same, jnp.concatenate([x] * heads, axis=1), 0.0)

    def gather(x):
        x = jnp.where(same, x, 0.0)
        y = x[:, :half_tok]
        for h in range(1, heads):
            y = y + x[:, h * half_tok:(h + 1) * half_tok]
        return y

    halves = range(2)
    here = [slice(h * (rows - keys), h * (rows - keys) + keys) for h in halves]
    q_cols = [spread(q_t[:, h * half_tok:(h + 1) * half_tok]) for h in halves]
    b_cols = [spread(b_t[:, h * half_tok:(h + 1) * half_tok]) for h in halves]
    p, inv_sum, parts, kt, vt = [], [], [], [], []
    for h, bias_ref in enumerate((bias0_ref, bias1_ref)):
        bias = bias_ref[0]
        s = dot(k_s[here[h], :], right6(split3(q_cols[h])))
        s = s + jnp.concatenate([bias] * (cols // bias.shape[1]), axis=1)
        p.append(jnp.exp(s - jnp.max(s, axis=0, keepdims=True)))
        kt.append(k_s[here[h], GROUP:3 * GROUP].T)
        vt.append(v_s[here[h], GROUP:3 * GROUP].T)
    for h in halves:
        inv_sum.append(1.0 / jnp.sum(p[h], axis=0, keepdims=True))
        parts.append(split(p[h]))
        b_cols[h] = b_cols[h] * inv_sum[h]
    mixed_parts, dp = [], []
    for h in halves:
        dp.append(dot(v_s[here[h], :], right6(split3(b_cols[h]))))
        m2 = dot(vt[h], parts[h][0])
        mixed_parts.append(gather((m2[:GROUP] + m2[GROUP:] + dot(vt[h][:GROUP], parts[h][1])) * inv_sum[h]))
    ds = []
    for h in halves:
        agreement = jnp.sum(p[h] * dp[h], axis=0, keepdims=True) * inv_sum[h]
        ds.append(split(p[h] * (dp[h] - agreement)))
        b_rows = split(b_cols[h].T)
        dv2 = dot(parts[h][0], jnp.concatenate(b_rows, axis=1))
        dkv_s[here[h], GROUP:] += dv2[:, :GROUP] + dv2[:, GROUP:] + dot(parts[h][1], b_rows[0])
    dq_parts = []
    for h in halves:
        q_rows = split(q_cols[h].T)
        dk2 = dot(ds[h][0], jnp.concatenate(q_rows, axis=1))
        dkv_s[here[h], :GROUP] += dk2[:, :GROUP] + dk2[:, GROUP:] + dot(ds[h][1], q_rows[0])
        dq2 = dot(kt[h], ds[h][0])
        dq_parts.append(gather(dq2[:GROUP] + dq2[GROUP:] + dot(kt[h][:GROUP], ds[h][1])))
    mixed_t = jnp.concatenate(mixed_parts, axis=1)
    dq = split((jnp.concatenate(dq_parts, axis=1) * scale).T)
    out_ref[...] += dot(left3(split(mixed_t.T)), right3(wo))
    cot = (c_s[:, :D], c_s[:, 2 * D:3 * D])
    gwo = dot(left3(split(mixed_t)), right3(cot))
    gq = dot(ot_s[...], right3(dq))
    dkv = split(dkv_s[...])
    gkv = dot(nt_s[...], right3(dkv))
    copies = [
        pltpu.make_async_copy(
            g_s.at[i % 2], (send_ref, keep_ref)[i // 2].at[pl.ds(i % 2 * 4 * D, 4 * D)], sems.at[i]
        )
        for i in range(4)
    ]
    for i in range(2):
        @pl.when(step == i + 2)
        def _(i=i):
            copies[i].wait()
    slot = step % 2
    g_s[slot, 0:D, :] = gq
    g_s[slot, D:2 * D, :] = gkv[:, :GROUP]
    g_s[slot, 2 * D:3 * D, :] = gkv[:, GROUP:]
    for j in range(D // GROUP):
        g_s[slot, 3 * D + j * GROUP:3 * D + (j + 1) * GROUP, :] = gwo[:, j * GROUP:(j + 1) * GROUP]
    for i in range(4):
        @pl.when(step == i)
        def _(i=i):
            copies[i].start()

    bn_s[...] += dot(left3((dkv[0][:rows], dkv[1][:rows])), right3(wkv, 1), 1, 1)
    back_q = dot(left3(dq), right3(wq, 1), 1, 1)
    for i in range(mid_lats):
        at = (LAT_REACH + i) * SLAB
        bn_s[at:at + 16, :] += back_q[i * 16:(i + 1) * 16]

    @pl.when(step == last)
    def _():
        bn3 = bn_s[...].reshape(lats, SLAB, D)
        btop_ref[...] = bn3[:LAT_REACH]
        bbot_ref[...] = bn3[LAT_REACH + mid_lats:]
        bmid_ref[...] = bn3[LAT_REACH:LAT_REACH + mid_lats]
        x = x_s[...]
        inv = lax.rsqrt(jnp.mean(x * x, axis=-1, keepdims=True) + EPSILON)
        gg = jnp.sum(bn_s[...] * (x * inv), axis=0, keepdims=True)
        t_s[...] = jnp.zeros(t_s.shape, F32)
        for j in range(D // GROUP):
            t_s[1, j:j + 1, :] = gg[:, j * GROUP:(j + 1) * GROUP]
        tails = [
            pltpu.make_async_copy(t_s.at[i], ref.at[pl.ds(8 * D, TAIL)], sems.at[4 + i])
            for i, ref in enumerate((send_ref, keep_ref))
        ]
        for copy in tails:
            copy.start()
        for copy in tails + copies[2:]:
            copy.wait()


def attention(pos, top, mid, bot, gain, w_qkv, w_out, cot, bias):
    mid_lats = mid.shape[0]
    lats = mid_lats + 2 * LAT_REACH
    rows = lats * SLAB
    tok = mid_lats * 16
    padded = -(-rows // 256) * 256
    groups = D // GROUP
    whole = lambda *shape: pl.BlockSpec(shape, lambda s, pos: (0,) * len(shape))
    slab = lambda n: whole(n, SLAB, D)
    like = lambda *shape: jax.ShapeDtypeStruct(shape, F32)
    group = lambda s, pos: 2 * (s % 2) + jnp.where(s < 2, 1 - pos[0], pos[0])
    outs, out_specs = [like(tok, D)], [whole(tok, D)]
    for n in (LAT_REACH, mid_lats, LAT_REACH):
        outs.append(like(n, SLAB, D))
        out_specs.append(slab(n))
    for _ in range(2):
        outs.append(like(8 * D + TAIL, GROUP))
        out_specs.append(pl.BlockSpec(memory_space=pl.ANY))
    return pl.pallas_call(
        attention_kernel,
        grid_spec=pltpu.PrefetchScalarGridSpec(
            num_scalar_prefetch=1,
            grid=(4,),
            in_specs=[
                slab(LAT_REACH), slab(mid_lats), slab(LAT_REACH), whole(1, D),
                pl.BlockSpec((D, GROUP), lambda s, pos: (0, group(s, pos))),
                pl.BlockSpec((D, GROUP), lambda s, pos: (0, groups + group(s, pos))),
                pl.BlockSpec((D, GROUP), lambda s, pos: (0, 2 * groups + group(s, pos))),
                pl.BlockSpec((GROUP, D), lambda s, pos: (group(s, pos), 0)),
                whole(tok, D),
                pl.BlockSpec((1,) + bias.shape[1:], lambda s, pos: (pos[1], 0, 0)),
                pl.BlockSpec((1,) + bias.shape[1:], lambda s, pos: (pos[2], 0, 0)),
            ],
            out_specs=out_specs,
            scratch_shapes=[
                pltpu.VMEM((rows, D), F32),
                pltpu.VMEM((rows, 6 * D), BF16), pltpu.VMEM((D, 3 * padded), BF16),
                pltpu.VMEM((tok, 6 * D), BF16), pltpu.VMEM((D, 3 * tok), BF16),
                pltpu.VMEM((tok, 6 * D), BF16),
                pltpu.VMEM((rows, D), F32), pltpu.VMEM((padded, 2 * GROUP), F32),
                pltpu.VMEM((rows, 6 * GROUP), BF16), pltpu.VMEM((rows, 6 * GROUP), BF16),
                pltpu.VMEM((2, 4 * D, GROUP), F32), pltpu.VMEM((2, TAIL, GROUP), F32),
                pltpu.SemaphoreType.DMA((6,)),
            ],
        ),
        out_shape=outs,
        compiler_params=pltpu.CompilerParams(vmem_limit_bytes=58 * 1024 * 1024),
        cost_estimate=pl.CostEstimate(flops=20_000_000_000, bytes_accessed=24_000_000, transcendentals=2_000_000),
        name="attention",
    )(pos, top, mid, bot, gain.reshape(1, D), w_qkv, w_qkv, w_qkv, w_out, cot, bias, bias)


def unpack_kernel(factor, core_ref, mine_ref, other_ref, gain_ref, qkv_ref, out_ref):
    groups = D // GROUP
    core = core_ref[0]
    for ref, keeper in ((mine_ref, core), (other_ref, 1 - core)):
        for k in range(2):
            g = 2 * k + keeper
            for j in range(3):
                cols = pl.ds(pl.multiple_of((j * groups + g) * GROUP, GROUP), GROUP)
                qkv_ref[:, cols] = ref[(4 * k + j) * D:(4 * k + j + 1) * D, :] * factor
            for j in range(groups):
                at = (4 * k + 3) * D + j * GROUP
                out_ref[g, :, j * GROUP:(j + 1) * GROUP] = ref[at:at + GROUP, :] * factor
    for row in range(D // GROUP):
        at = 8 * D + row
        gain_ref[row:row + 1, :] = (mine_ref[at:at + 1, :] + other_ref[at:at + 1, :]) * factor


def unpack(core, factor, mine, other):
    return pl.pallas_call(
        lambda *refs: unpack_kernel(factor, *refs),
        in_specs=[pl.BlockSpec(memory_space=pltpu.SMEM)] + [pl.BlockSpec(memory_space=pltpu.VMEM)] * 2,
        out_specs=[pl.BlockSpec(memory_space=pltpu.VMEM)] * 3,
        out_shape=[
            jax.ShapeDtypeStruct((D // GROUP, GROUP), F32),
            jax.ShapeDtypeStruct((D, 3 * D), F32),
            jax.ShapeDtypeStruct((D // GROUP, GROUP, D), F32),
        ],
        compiler_params=pltpu.CompilerParams(vmem_limit_bytes=32 * 1024 * 1024),
        cost_estimate=pl.CostEstimate(flops=1_000_000, bytes_accessed=8_000_000, transcendentals=0),
        name="unpack",
    )(core, mine, other)


def shift(x, axis, step, closed):
    count = lax.axis_size(axis)
    ends = count if closed else count - 1
    pairs = [(i, (i + 1) % count) for i in range(ends)]
    if step < 0:
        pairs = [(j, i) for i, j in pairs]
    return lax.ppermute(x, axis, pairs)


def shift_across(x, step):
    count = lax.axis_size("lon")
    pairs = []
    for i in range(count):
        for e in range(2):
            pairs.append((i * 2 + e, ((i + step) % count) * 2 + 1 - e))
    return lax.ppermute(x, ("lon", "lev"), pairs)


def swap_lev(x):
    return lax.ppermute(x, "lev", [(0, 1), (1, 0)])


def window_bias(lat_dev, lon_dev, keys):
    left = np.arange(-LON_REACH, 0)
    right = np.arange(lon_dev, lon_dev + LON_REACH)
    lon = np.concatenate([
        np.repeat(np.arange(lon_dev), 2), np.arange(lon_dev), np.repeat(left, 2), left,
        np.repeat(right, 2), right,
    ])
    level = np.concatenate([
        np.tile([0, 1], lon_dev), np.full(lon_dev, 2), np.tile([0, 1], LON_REACH),
        np.full(LON_REACH, 2), np.tile([0, 1], LON_REACH), np.full(LON_REACH, 2),
    ])
    unused = SLAB - lon.shape[0]
    lon = np.concatenate([lon, np.full(unused, 1000)])
    level = np.concatenate([level, np.full(unused, 0)])
    lats = lat_dev + 2 * LAT_REACH
    rows = lats * SLAB
    lat = np.repeat(np.arange(lats) - LAT_REACH, SLAB)[:, None]
    lon = np.tile(lon, lats)[:, None]
    level = np.tile(level, lats)[:, None]
    q_lat = np.repeat(np.arange(lat_dev), lon_dev * 2)
    q_lon = np.tile(np.repeat(np.arange(lon_dev), 2), lat_dev)
    q_level = np.tile([0, 1], lat_dev * lon_dev)
    near = (np.abs(lat - q_lat) <= LAT_REACH) & (np.abs(lon - q_lon) <= LON_REACH)
    half = q_lat.shape[0] // 2
    table = []
    for part in range(2):
        first = part * (rows - keys)
        ks = slice(first, first + keys)
        qs = np.tile(np.arange(part * half, (part + 1) * half), 2)
        for side in range(2):
            lev_k = np.where(level == 2, 2 - side, side * 2 + level)
            seen = near & (np.abs(lev_k - (side * 2 + q_level)) <= LEV_REACH)
            for edge in range(2):
                kept = seen
                if edge == 1:
                    kept = seen & ((lat >= 0) if part == 0 else (lat < lat_dev))
                table.append(np.where(kept[ks][:, qs], 0.0, NEVER))
    return np.stack(table).astype(np.float32)


def bit_of(axis, bit):
    return (lax.axis_index(axis) >> bit) & 1


def swap_bit(x, axis, bit):
    return lax.ppermute(x, axis, [(i, i ^ (1 << bit)) for i in range(lax.axis_size(axis))])


def halve(blocks, bits):
    def half(block, which):
        terms, start, size = block
        n = size // 2
        return sum(lax.dynamic_slice_in_dim(x, start + which * n, n, 0) for x in terms)

    mine = [bit_of(*bit) for bit in bits]
    given = [half(x, 1 - m) for x, m in zip(blocks, mine)]
    came = [swap_bit(x, *bit) for x, bit in zip(given, bits)]
    if len(came) > 1:
        came = [after(x, given) for x in came]
    kept = [((half(x, m) + s,), 0, s.shape[0]) for x, m, s in zip(blocks, mine, came)]
    return kept


def double(blocks, bits):
    came = [after(swap_bit(x, *bit), blocks) for x, bit in zip(blocks, bits)]
    grown = []
    for x, s, (axis, bit) in zip(blocks, came, bits):
        mine = bit_of(axis, bit) == 1
        grown.append([jnp.where(mine, s, x), jnp.where(mine, x, s)])
    return grown


def bits_in(axis):
    count = lax.axis_size(axis)
    assert count & (count - 1) == 0
    return [(axis, b) for b in range(count.bit_length() - 1)]


def after(x, done):
    return lax.optimization_barrier((x, done))[0]


def finish_kernel(low_ref, back_ref, left_ref, right_ref, edge_ref, x_ref, cot_ref, gain_ref, out_ref):
    r = LON_REACH
    lats, lons = edge_ref.shape[:2]
    low = low_ref[0]
    row = lax.broadcasted_iota(jnp.int32, (2 * lons, lons), 0)
    col = lax.broadcasted_iota(jnp.int32, (2 * lons, lons), 1)
    place = jnp.where(row == 2 * col + low, 1.0, 0.0).astype(F32)
    cells = lax.broadcasted_iota(jnp.int32, (2 * lons, 1), 0)
    gain = gain_ref[...]
    for i in range(lats):
        total = back_ref[i, :16, :]
        none = jnp.zeros((16 - 2 * r, D), F32)
        total = total + jnp.concatenate([none, left_ref[i, :2 * r, :]], axis=0)
        total = total + jnp.concatenate([right_ref[i, :2 * r, :], none], axis=0)
        total = total + jnp.dot(place, edge_ref[i], precision=lax.Precision.HIGHEST, preferred_element_type=F32)
        x = x_ref[i]
        inv_rms = lax.rsqrt(jnp.mean(x * x, axis=-1, keepdims=True) + EPSILON)
        scaled = gain * total
        grad = cot_ref[i * 16:(i + 1) * 16, :] + inv_rms * scaled
        dots = jnp.mean(scaled * x, axis=-1, keepdims=True)
        out_ref[i * 16:(i + 1) * 16, :] = grad - x * (inv_rms * inv_rms * inv_rms * dots)


def finish(low, back, to_left, to_right, edge_sum, own, cot, gain):
    vmem = pl.BlockSpec(memory_space=pltpu.VMEM)
    return pl.pallas_call(
        finish_kernel,
        in_specs=[pl.BlockSpec(memory_space=pltpu.SMEM)] + [vmem] * 7,
        out_specs=vmem,
        out_shape=jax.ShapeDtypeStruct(cot.shape, F32),
        compiler_params=pltpu.CompilerParams(vmem_limit_bytes=16 * 1024 * 1024),
        cost_estimate=pl.CostEstimate(flops=3_000_000, bytes_accessed=3_000_000, transcendentals=0),
        name="finish",
    )(low.astype(jnp.int32).reshape(1), back, to_left, to_right, edge_sum, own, cot, gain.reshape(1, D))


def per_device(fields, gain, w_qkv, w_out, cotangent):
    lat_dev, lon_dev, lev_dev = fields.shape[:3]
    assert lev_dev == 2 and lax.axis_size("lev") == 2 and lon_dev * lev_dev == 16
    tok = lat_dev * lon_dev * lev_dev
    low = lax.axis_index("lev") == 0
    r = LON_REACH
    edge = jnp.where(low, fields[:, :, 1], fields[:, :, 0])
    own = fields.reshape(lat_dev, 16, D)
    left_own = shift(own[:, 16 - 2 * r:], "lon", 1, True)
    right_own = shift(own[:, :2 * r], "lon", -1, True)
    left_far = shift_across(edge[:, lon_dev - r:], 1)
    right_far = shift_across(edge[:, :r], -1)
    far = swap_lev(edge)
    blank = jnp.zeros((lat_dev, SLAB - 24 - 6 * r, D), F32)
    mid = jnp.concatenate([own, far, left_own, left_far, right_own, right_far, blank], axis=1)
    top = shift(mid[lat_dev - LAT_REACH:], "lat", 1, False)
    bot = shift(mid[:LAT_REACH], "lat", -1, False)
    bias = jnp.asarray(window_bias(lat_dev, lon_dev, 512))
    lat_id, lev_id = lax.axis_index("lat"), lax.axis_index("lev")
    core = lat_id & 1
    pos = jnp.stack([
        core, lev_id * 2 + (lat_id == 0), 4 + lev_id * 2 + (lat_id == lax.axis_size("lat") - 1),
    ]).astype(jnp.int32)
    shared = (gain, w_qkv, w_out, cotangent.reshape(tok, D), bias)
    out, btop, bmid, bbot, send, keep = attention(pos, top, mid, bot, *shared)
    from_low = shift(bbot, "lat", 1, False)
    from_high = shift(btop, "lat", -1, False)
    (pair,), x_bits = bits_in("lat")[:1], bits_in("lat")[1:]
    y_bits, z_bits = bits_in("lev"), bits_in("lon")
    zh_bits = z_bits[:-1]
    orders = [x_bits + y_bits + zh_bits, y_bits + zh_bits + x_bits, zh_bits + x_bits + y_bits]
    stages = len(orders[0])
    total = (keep, swap_bit(send, *pair))
    blocks, at, unit = [], 0, (8 * D + TAIL) // TAIL
    for i in range(3):
        size = (unit + 2 - i) // 3 * TAIL
        blocks.append((total, at, size))
        at += size
    rest = lat_dev - LAT_REACH
    low_at, high_at = 24, 24 + 3 * r
    for stage in range(stages):
        blocks = halve(blocks, [order[stage] for order in orders])
        if stage == 0:
            tied = lax.optimization_barrier(([x[0] for x in blocks], from_low, from_high))
            blocks = [(t,) + x[1:] for t, x in zip(tied[0], blocks)]
            back = bmid + jnp.pad(tied[1], ((0, rest), (0, 0), (0, 0)))
            back = back + jnp.pad(tied[2], ((rest, 0), (0, 0), (0, 0)))
            to_left = shift(back[:, low_at:high_at], "lon", -1, True)
            to_right = shift(back[:, high_at:high_at + 3 * r], "lon", 1, True)
    sizes = [x[2] for x in blocks]
    every = jnp.concatenate([x[0][0] for x in blocks], axis=0)
    every, to_left, to_right = lax.optimization_barrier((every, to_left, to_right))
    every = every + swap_bit(every, *z_bits[-1])
    other = back[:, 16:24] + jnp.pad(to_left[:, 2 * r:], ((0, 0), (lon_dev - r, 0), (0, 0)))
    other = other + jnp.pad(to_right[:, 2 * r:], ((0, 0), (0, lon_dev - r), (0, 0)))
    every, edge_sum = lax.optimization_barrier((every, swap_lev(other)))
    grad_fields = finish(
        low, back, to_left, to_right, edge_sum, own, cotangent.reshape(tok, D), gain
    ).reshape(fields.shape)
    blocks = [every[:sizes[0]], every[sizes[0]:sizes[0] + sizes[1]], every[sizes[0] + sizes[1]:]]
    for stage in reversed(range(stages)):
        if stage == 0:
            blocks[0] = after(blocks[0], grad_fields)
        parts = double(blocks, [order[stage] for order in orders])
        if stage > 0:
            blocks = [jnp.concatenate(x, axis=0) for x in parts]
    mine = jnp.concatenate(parts[0] + parts[1] + parts[2], axis=0)
    devices = lax.axis_size("lat") * lax.axis_size("lon") * lax.axis_size("lev")
    factor = (tok * devices) ** (-0.5)
    grad_gain, grad_qkv, grad_out = unpack(
        core.reshape(1).astype(jnp.int32), factor,
        mine, swap_bit(mine, *pair),
    )
    grad_gain, grad_out = grad_gain.reshape(D), grad_out.reshape(D, D)
    return (out.reshape(fields.shape), grad_fields, grad_gain, grad_qkv, grad_out)


def solution(mesh):
    cells = P("lat", "lon", "lev", None)
    return jax.shard_map(
        per_device, mesh=mesh, in_specs=(cells, P(), P(), P(), cells),
        out_specs=(cells, cells, P(), P(), P()), check_vma=False,
    )
```
